512 devices in a mesh: dp: 32 (over y_lo, z), owner: 16 (over y_hi, x, core).
Axes of the slice: x: 4, y: 4 (y_hi: 2, y_lo: 2; y = y_hi * 2 + y_lo), z: 16, core: 2. Of those that a mesh axis runs over, the one named last changes fastest.
Arguments:
- tokens: bfloat16 [4096, 4096], P('dp'), may hold values from -6 to 6
- act_basis: bfloat16 [2, 4096, 4096], P(None, 'dp', 'owner'), may hold values from -0.09375 to 0.09375
- grad_basis: bfloat16 [2, 8192, 8192], P(None, 'owner', 'dp'), may hold values from -0.0625 to 0.0625
- grads: bfloat16 [2, 4096, 8192], P(None, 'dp', 'owner'), may hold values from -6 to 6
- expert_ids: int32 [4096, 2], P('dp'), may hold values from 0 to 7, all different within a row; in each aligned block of 128 rows (0 to 127, 128 to 255, ...) at most 64 rows name the same one
Outputs:
- corrected: float32 [2, 8192, 4096], P(None, 'dp', 'owner')
The draws below stay inside these ranges and needn't reach their ends.
Inputs may be any that keep to these rules, and one draw needn't show every extreme that they name: `expert_ids`: among the 128 rows of one device no expert is named by more than 64 rows, a bound that some block reaches; the two experts of a row differ.
All inputs are finite; a program needn't handle non-finite values.
Results may differ from the reference program's by a relative error of at most 0.0013.
Values may be sent and summed in bfloat16 or wider, within the bound.
No kernel may reach another device: no remote copies, remote signals or barrier semaphores. Data moves between devices by JAX's collectives and lax.ppermute only.
A program may use at most 64 MiB of HBM per device.

```python
import math
import jax
import jax.numpy as jnp
import numpy as np

D = 4096
EXPERTS = 8
TOPK = 2
FF_WIN = 8192
EXP_WIN = 2
TOK_DEV = 128
CAP = 64
ROWS = 2048
TOKENS = 4096
N_DP = 32


def block_scale(stream_key, extent, shards, smallest, largest):
    loudness, own = 1.0, jax.random.fold_in(stream_key, 6)
    for axis_at, shards_of in shards:
        steps = jnp.exp(jax.random.uniform(jax.random.fold_in(own, axis_at), (shards_of,), jnp.float32, smallest / len(shards), largest / len(shards)))
        loudness = loudness * jnp.repeat(steps, extent[axis_at] // shards_of).reshape([-1 if axis == axis_at else 1 for axis in range(len(extent))])
    return loudness


def deal_out(own_key, own, number, rows, number_of, top, most, skew):
    order = jax.random.permutation(own_key, number_of)
    packed, common = load_shares(number_of, rows * top, most, skew, True), load_shares(number_of, rows * top, most, skew, False)
    places = jnp.arange(number_of)

    def named(tallies, offset_by):
        used = int((tallies > 0).sum())
        fixed = max(1, used // 4)
        passed = fixed + (places - fixed + offset_by * (used - fixed)) % max(1, number_of - fixed)
        return jnp.zeros((number_of,), jnp.int32).at[order[jnp.where(places < fixed, places, passed)]].set(jnp.asarray(tallies, jnp.int32))

    tallies = jnp.where(number % 4 == 0, named(packed, number // 4), named(common, number - number // 4 - 1))
    mixed = jax.random.permutation(jax.random.fold_in(own, 3), number_of)
    source_of, taker = mixed[0:number_of // 2 * 2:2], mixed[1:number_of // 2 * 2:2]
    margin = jnp.minimum(tallies[source_of] - 1, most - tallies[taker]) // 2
    margin = jnp.where((source_of == order[0]) | (taker == order[0]) | (tallies[taker] == 0), 0, jnp.maximum(margin, 0))
    passed = jax.random.randint(jax.random.fold_in(own, 4), (number_of // 2,), 0, 1 << 20) % (margin + 1)
    tallies = tallies.at[source_of].add(-passed).at[taker].add(passed)
    labels = jnp.searchsorted(jnp.cumsum(tallies), jnp.arange(rows * top), side="right").astype(jnp.int32)
    table = labels.reshape(top, rows).T
    table = table[jax.random.permutation(jax.random.fold_in(own, 1), rows)]
    offset_by = jax.random.randint(jax.random.fold_in(own, 2), (rows, 1), 0, top)
    return jnp.take_along_axis(table, (jnp.arange(top)[None, :] + offset_by) % top, axis=1)


def load_shares(count, total, reach, lean, full):
    portions = [(1 << 20) // math.isqrt(grade ** lean) + 1 for grade in range(1, count + 1)]
    largest = reach if full else min(reach, max(-(-total // count), total * portions[0] // sum(portions)))
    least = 1 if total - largest >= count - 1 else 0
    given, spare = [largest] + [least] * (count - 1), total - largest - least * (count - 1)
    while spare > 0:
        candidates = [i for i in range(1, count) if given[i] < largest] or [i for i in range(1, count) if given[i] < reach]
        whole, left = sum([portions[i] for i in candidates]), spare
        for i in candidates:
            extra = min(reach - given[i], max(1, left * portions[i] // whole), spare)
            given[i] = given[i] + extra
            spare = spare - extra
    return np.array(given)


def centred(stream_key, shape, scale, limit, split=(), kind=jnp.bfloat16):
    entries = scale * jax.random.normal(stream_key, shape, jnp.float32)
    if split:
        entries = entries * block_scale(stream_key, shape, split, -0.22, 0.18)
    return jnp.clip(entries, -limit, limit).astype(kind)


def setup_inputs(seed: int = 0) -> dict:
    keys = jax.random.split(jax.random.key(seed), 6)
    tokens = centred(keys[0], (TOKENS, D), 1.0, 6.0, ((0, 32),))
    act_basis = centred(keys[1], (EXP_WIN, D, D), D ** -0.5, 0.09375, ((1, 32), (2, 16)))
    grad_basis = centred(keys[2], (EXP_WIN, FF_WIN, FF_WIN), FF_WIN ** -0.5, 0.0625, ((1, 16), (2, 32)))
    grads = centred(keys[3], (EXP_WIN, TOKENS, FF_WIN), 1.0, 6.0, ((1, 32), (2, 16)))
    expert_ids_keys = jax.random.split(jax.random.fold_in(keys[4], 1), TOKENS // TOK_DEV)
    expert_ids_turns = jax.random.permutation(jax.random.fold_in(keys[4], 3), TOKENS // TOK_DEV)
    expert_ids = jax.vmap(lambda own, number: deal_out(jax.random.fold_in(keys[4], 2), own, number, TOK_DEV, EXPERTS, TOPK, CAP, 2))(expert_ids_keys, expert_ids_turns).reshape((TOKENS, TOPK))
    return dict(tokens=tokens, act_basis=act_basis, grad_basis=grad_basis, grads=grads, expert_ids=expert_ids)


def reference(tokens, act_basis, grad_basis, grads, expert_ids):
    token_groups = tokens.reshape(N_DP, TOK_DEV, D).astype(jnp.float32)
    id_groups = expert_ids.reshape(N_DP, TOK_DEV, TOPK)
    slot_order = jnp.arange(CAP, dtype=jnp.int32)
    results = []
    for expert in range(EXP_WIN):
        routed = jnp.any(id_groups == expert, axis=2)
        slot_index = jnp.cumsum(routed.astype(jnp.int32), axis=1) - 1
        chooser = jnp.logical_and(routed[:, None, :], slot_index[:, None, :] == slot_order[None, :, None]).astype(jnp.float32)
        picked_act = jnp.einsum('gct,gtd->gcd', chooser, token_groups).reshape(ROWS, D).astype(jnp.bfloat16)
        grad_groups = grads[expert].reshape(N_DP, TOK_DEV, FF_WIN).astype(jnp.float32)
        picked_grad = jnp.einsum('gct,gtf->gcf', chooser, grad_groups).reshape(ROWS, FF_WIN).astype(jnp.bfloat16)
        act_proj = jnp.dot(picked_act, act_basis[expert], preferred_element_type=jnp.float32).astype(jnp.bfloat16)
        grad_proj = jnp.dot(picked_grad, grad_basis[expert], preferred_element_type=jnp.float32)
        act_sq = jnp.square(act_proj.astype(jnp.float32)).astype(jnp.bfloat16)
        grad_sq = jnp.square(grad_proj).astype(jnp.bfloat16)
        results.append(jnp.dot(grad_sq.T, act_sq, preferred_element_type=jnp.float32) / TOKENS)
    return jnp.stack(results)
```

```python
import jax
import jax.numpy as jnp
from jax import lax
from jax.sharding import Mesh, PartitionSpec as P

F32, BF16 = jnp.float32, jnp.bfloat16
PLANE = ("yh", "x")


def choosers(expert_ids, experts, capacity):
    slot_order = jnp.arange(capacity, dtype=jnp.int32)[:, None]
    rows = expert_ids.shape[0]
    before = jnp.tril(jnp.ones((rows, rows), BF16))
    out = []
    for expert in range(experts):
        routed = jnp.any(expert_ids == expert, axis=1)
        count = jnp.dot(before, routed.astype(BF16)[:, None], preferred_element_type=F32)[:, 0]
        slot_index = count.astype(jnp.int32) - 1
        chosen = jnp.logical_and(routed[None, :], slot_index[None, :] == slot_order)
        out.append(chosen.astype(BF16))
    return out


def pick(chooser, rows):
    return jnp.dot(chooser, rows, preferred_element_type=F32).astype(BF16)


def swap(x, axis):
    return lax.ppermute(x, axis, [(0, 1), (1, 0)])


def dot(a, b):
    return jnp.dot(a, b, preferred_element_type=F32)


def per_device(tokens, act_basis, grad_basis, grads, expert_ids):
    tok_rows, width = tokens.shape
    capacity = tok_rows // 2
    nz = lax.axis_size("z")
    token_total = tok_rows * lax.axis_size("yl") * nz
    planes = lax.axis_size("yh") * lax.axis_size("x")
    yl, core = lax.axis_index("yl"), lax.axis_index("c")
    basis_rows, cols = act_basis.shape[1:]
    hidden = grads.shape[2]

    def mine(x):
        return lax.dynamic_index_in_dim(x, yl, 0, keepdims=False)

    def theirs(x):
        return lax.dynamic_index_in_dim(x, 1 - yl, 0, keepdims=False)

    act_other = swap(theirs(act_basis), "yl")
    choose = choosers(expert_ids, 2, capacity)
    picked_grad = jnp.stack([pick(choose[e], grads[e]) for e in range(2)])
    straight = [(2 * y + c, 2 * c + y) for y in range(2) for c in range(2)]
    crossed = [(2 * y + c, 2 * (1 - c) + y) for y in range(2) for c in range(2)]
    grad_a = lax.ppermute(
        lax.dynamic_index_in_dim(picked_grad, core, 0, keepdims=False), ("yl", "c"), straight
    )
    grad_b = lax.ppermute(
        lax.dynamic_index_in_dim(picked_grad, 1 - core, 0, keepdims=False), ("yl", "c"), crossed
    )
    act_rows = jnp.concatenate([mine(act_basis), act_other], axis=1)
    payload = jnp.concatenate([act_rows, grad_a, grad_b], axis=0)
    gathered = lax.all_gather(payload, "z", axis=0, tiled=False)

    picked_act = jnp.stack([pick(choose[e], tokens) for e in range(2)])
    act_in, act_in_other = mine(picked_act), swap(theirs(picked_act), "yl")
    first = jnp.where(yl == core, act_in, act_in_other)
    second = jnp.where(yl == core, act_in_other, act_in)
    rows = jnp.concatenate([first, second], axis=0)
    low, high = rows[:, : width // 2], rows[:, width // 2 :]
    rows_own = jnp.where(yl == 0, low, high)
    rows_other = jnp.where(yl == 0, high, low)
    basis_half = jnp.concatenate([mine(grad_basis), swap(theirs(grad_basis), "yl")], axis=1)
    basis_peer = swap(basis_half, "c")
    basis_a = jnp.where(yl == core, basis_half, basis_peer)
    basis_b = jnp.where(yl == core, basis_peer, basis_half)

    own_basis = gathered[:, :basis_rows, :cols].reshape(nz * basis_rows, cols)
    other_basis = gathered[:, :basis_rows, cols:].reshape(nz * basis_rows, cols)
    act_proj = (dot(rows_own, own_basis) + dot(rows_other, other_basis)).astype(BF16)
    act_all = lax.all_gather(act_proj, "z", axis=0, tiled=False)

    got_a = gathered[:, basis_rows : basis_rows + capacity].reshape(nz * capacity, hidden)
    got_b = gathered[:, basis_rows + capacity :].reshape(nz * capacity, hidden)
    part = dot(got_a, basis_a) + dot(got_b, basis_b)
    share = part.shape[0] // planes
    parts = lax.all_to_all(part.reshape(planes, share, -1), PLANE, 0, 0, tiled=True)
    grad_sq = jnp.square(jnp.sum(parts, axis=0)).astype(BF16)
    copies = jnp.broadcast_to(grad_sq[None], (planes,) + grad_sq.shape)
    grad_sq = lax.all_to_all(copies, PLANE, 0, 0, tiled=True).reshape(nz * capacity, -1)
    grad_sq_other = swap(grad_sq, "c")

    act_sq = jnp.square(act_all.astype(F32)).astype(BF16)
    act_first = act_sq[:, :capacity].reshape(nz * capacity, cols)
    act_second = act_sq[:, capacity:].reshape(nz * capacity, cols)

    def outer(g, a):
        return lax.dot_general(g, a, (((0,), (0,)), ((), ())), preferred_element_type=F32)

    block = (outer(grad_sq, act_first) + outer(grad_sq_other, act_second)) / token_total
    half = block.shape[0] // 2
    kept, got = block[:half], swap(block[half:], "yl")
    return jnp.stack([jnp.where(yl == 0, kept, got), jnp.where(yl == 0, got, kept)])


def solution(mesh):
    dp, owner = mesh.devices.shape
    split = Mesh(mesh.devices.reshape(2, dp // 2, 2, owner // 4, 2), ("yl", "z", "yh", "x", "c"))
    rows, cols = ("yl", "z"), ("yh", "x", "c")
    placed = (
        P(rows, None),
        P(None, rows, cols),
        P(None, cols, rows),
        P(None, rows, cols),
        P(rows, None),
    )
    return jax.shard_map(
        per_device, mesh=split, in_specs=placed, out_specs=P(None, rows, cols), check_vma=False
    )
```

```python
import jax
import jax.numpy as jnp
from jax import lax
from jax.sharding import Mesh, PartitionSpec as P

F32, BF16 = jnp.float32, jnp.bfloat16
PLANE = ("yh", "x")


def choosers(expert_ids, experts, capacity):
    slot_order = jnp.arange(capacity, dtype=jnp.int32)[:, None]
    rows = expert_ids.shape[0]
    before = jnp.tril(jnp.ones((rows, rows), BF16))
    out = []
    for expert in range(experts):
        routed = jnp.any(expert_ids == expert, axis=1)
        count = jnp.dot(before, routed.astype(BF16)[:, None], preferred_element_type=F32)[:, 0]
        slot_index = count.astype(jnp.int32) - 1
        chosen = jnp.logical_and(routed[None, :], slot_index[None, :] == slot_order)
        out.append(chosen.astype(BF16))
    return out


def pick(chooser, rows):
    return jnp.dot(chooser, rows, preferred_element_type=F32).astype(BF16)


def swap(x, axis):
    return lax.ppermute(x, axis, [(0, 1), (1, 0)])


def dot(a, b):
    return jnp.dot(a, b, preferred_element_type=F32)


def per_device(tokens, act_basis, grad_basis, grads, expert_ids):
    tok_rows, width = tokens.shape
    capacity = tok_rows // 2
    nl = lax.axis_size("zl")
    nz = lax.axis_size("zh") * nl
    token_total = tok_rows * lax.axis_size("yl") * nz
    planes = lax.axis_size("yh") * lax.axis_size("x")
    yl, core = lax.axis_index("yl"), lax.axis_index("c")
    basis_rows, cols = act_basis.shape[1:]
    hidden = grads.shape[2]

    def mine(x):
        return lax.dynamic_index_in_dim(x, yl, 0, keepdims=False)

    def theirs(x):
        return lax.dynamic_index_in_dim(x, 1 - yl, 0, keepdims=False)

    act_other = swap(theirs(act_basis), "yl")
    choose = choosers(expert_ids, 2, capacity)
    picked_grad = jnp.stack([pick(choose[e], grads[e]) for e in range(2)])
    straight = [(2 * y + c, 2 * c + y) for y in range(2) for c in range(2)]
    crossed = [(2 * y + c, 2 * (1 - c) + y) for y in range(2) for c in range(2)]
    grad_a = lax.ppermute(
        lax.dynamic_index_in_dim(picked_grad, core, 0, keepdims=False), ("yl", "c"), straight
    )
    grad_b = lax.ppermute(
        lax.dynamic_index_in_dim(picked_grad, 1 - core, 0, keepdims=False), ("yl", "c"), crossed
    )
    act_rows = jnp.concatenate([mine(act_basis), act_other], axis=1)
    payload = jnp.concatenate([act_rows, grad_a, grad_b], axis=0)
    gathered = lax.all_gather(payload, ("zh", "zl"), axis=0, tiled=False)

    plane = lax.axis_index("yh") * lax.axis_size("x") + lax.axis_index("x")
    share = width // (2 * planes)
    piece = lax.dynamic_slice_in_dim(tokens, core * (width // 2) + plane * share, share, 1)
    picked_act = jnp.stack([pick(choose[e], piece) for e in range(2)])
    act_in, act_in_other = mine(picked_act), swap(theirs(picked_act), "yl")
    rows = jnp.concatenate(
        [jnp.where(yl == 0, act_in, act_in_other), jnp.where(yl == 0, act_in_other, act_in)], axis=0
    )
    rows = lax.all_gather(rows, "zh", axis=0, tiled=True)
    copies = jnp.broadcast_to(rows[None], (planes,) + rows.shape)
    rows = lax.all_to_all(copies, PLANE, 0, 0, tiled=True)
    rows = rows.transpose(1, 0, 2).reshape(rows.shape[1], planes * share)
    rows_peer = swap(rows, "c")
    rows_own = jnp.where(yl == core, rows, rows_peer)
    rows_other = jnp.where(yl == core, rows_peer, rows)
    basis_half = jnp.concatenate([mine(grad_basis), swap(theirs(grad_basis), "yl")], axis=1)
    basis_peer = swap(basis_half, "c")
    basis_a = jnp.where(yl == core, basis_half, basis_peer)
    basis_b = jnp.where(yl == core, basis_peer, basis_half)

    own_basis = gathered[:, :basis_rows, :cols].reshape(nz * basis_rows, cols)
    other_basis = gathered[:, :basis_rows, cols:].reshape(nz * basis_rows, cols)
    act_proj = (dot(rows_own, own_basis) + dot(rows_other, other_basis)).astype(BF16)
    got_a = gathered[:, basis_rows : basis_rows + capacity].reshape(nz * capacity, hidden)
    got_b = gathered[:, basis_rows + capacity :].reshape(nz * capacity, hidden)
    act_proj, got_a, got_b = lax.optimization_barrier((act_proj, got_a, got_b))
    act_all = lax.all_gather(act_proj, "zl", axis=0, tiled=False)

    part = dot(got_a, basis_a) + dot(got_b, basis_b)
    parts = lax.all_to_all(part.reshape(planes, part.shape[0] // planes, -1), PLANE, 0, 0, tiled=True)
    grad_sq = jnp.square(jnp.sum(parts, axis=0)).astype(BF16)
    copies = jnp.broadcast_to(grad_sq[None], (planes,) + grad_sq.shape)
    grad_sq = lax.all_to_all(copies, PLANE, 0, 0, tiled=True).reshape(nz * capacity, -1)
    grad_sq_other = swap(grad_sq, "c")

    act_sq = jnp.square(act_all.astype(F32)).astype(BF16)
    act_sq = act_sq.reshape(nl, nz // nl, 2, capacity, cols).transpose(2, 1, 0, 3, 4)
    act_sq = act_sq.reshape(2, nz * capacity, cols)
    act_first = lax.dynamic_index_in_dim(act_sq, core, 0, keepdims=False)
    act_second = lax.dynamic_index_in_dim(act_sq, 1 - core, 0, keepdims=False)

    def outer(g, a):
        return lax.dot_general(g, a, (((0,), (0,)), ((), ())), preferred_element_type=F32)

    block = (outer(grad_sq, act_first) + outer(grad_sq_other, act_second)) / token_total
    half = block.shape[0] // 2
    kept, got = block[:half], swap(block[half:], "yl")
    return jnp.stack([jnp.where(yl == 0, kept, got), jnp.where(yl == 0, got, kept)])


def solution(mesh):
    dp, owner = mesh.devices.shape
    split = Mesh(
        mesh.devices.reshape(2, dp // 8, 4, 2, owner // 4, 2), ("yl", "zh", "zl", "yh", "x", "c")
    )
    rows, cols = ("yl", "zh", "zl"), ("yh", "x", "c")
    placed = (
        P(rows, None),
        P(None, rows, cols),
        P(None, cols, rows),
        P(None, rows, cols),
        P(rows, None),
    )
    return jax.shard_map(
        per_device, mesh=split, in_specs=placed, out_specs=P(None, rows, cols), check_vma=False
    )
```

```python
import jax
import jax.numpy as jnp
from jax import lax
from jax.sharding import Mesh, PartitionSpec as P

F32, BF16 = jnp.float32, jnp.bfloat16
PLANE = ("yh", "x")


def choosers(expert_ids, experts, capacity):
    slot_order = jnp.arange(capacity, dtype=jnp.int32)[:, None]
    rows = expert_ids.shape[0]
    before = jnp.tril(jnp.ones((rows, rows), BF16))
    out = []
    for expert in range(experts):
        routed = jnp.any(expert_ids == expert, axis=1)
        count = jnp.dot(before, routed.astype(BF16)[:, None], preferred_element_type=F32)[:, 0]
        slot_index = count.astype(jnp.int32) - 1
        chosen = jnp.logical_and(routed[None, :], slot_index[None, :] == slot_order)
        out.append(chosen.astype(BF16))
    return out


def pick(chooser, rows):
    return jnp.dot(chooser, rows, preferred_element_type=F32).astype(BF16)


def swap(x, axis):
    return lax.ppermute(x, axis, [(0, 1), (1, 0)])


def dot(a, b):
    return jnp.dot(a, b, preferred_element_type=F32)


def per_device(tokens, act_basis, grad_basis, grads, expert_ids):
    tok_rows, width = tokens.shape
    capacity = tok_rows // 2
    nl = lax.axis_size("zl")
    nz = lax.axis_size("zh") * nl
    token_total = tok_rows * lax.axis_size("yl") * nz
    planes = lax.axis_size("yh") * lax.axis_size("x")
    yl, core = lax.axis_index("yl"), lax.axis_index("c")
    basis_rows, cols = act_basis.shape[1:]
    hidden = grads.shape[2]

    def mine(x):
        return lax.dynamic_index_in_dim(x, yl, 0, keepdims=False)

    def theirs(x):
        return lax.dynamic_index_in_dim(x, 1 - yl, 0, keepdims=False)

    act_other = swap(theirs(act_basis), "yl")
    choose = choosers(expert_ids, 2, capacity)
    picked_grad = jnp.stack([pick(choose[e], grads[e]) for e in range(2)])
    straight = [(2 * y + c, 2 * c + y) for y in range(2) for c in range(2)]
    crossed = [(2 * y + c, 2 * (1 - c) + y) for y in range(2) for c in range(2)]
    grad_a = lax.ppermute(
        lax.dynamic_index_in_dim(picked_grad, core, 0, keepdims=False), ("yl", "c"), straight
    )
    grad_b = lax.ppermute(
        lax.dynamic_index_in_dim(picked_grad, 1 - core, 0, keepdims=False), ("yl", "c"), crossed
    )
    act_rows = jnp.concatenate([mine(act_basis), act_other], axis=1)
    payload = jnp.concatenate([act_rows, grad_a, grad_b], axis=0)
    gathered = lax.all_gather(payload, ("zh", "zl"), axis=0, tiled=False)

    plane = lax.axis_index("yh") * lax.axis_size("x") + lax.axis_index("x")
    share = width // (2 * planes)
    piece = lax.dynamic_slice_in_dim(tokens, core * (width // 2) + plane * share, share, 1)
    picked_act = jnp.stack([pick(choose[e], piece) for e in range(2)])
    act_in, act_in_other = mine(picked_act), swap(theirs(picked_act), "yl")
    rows = jnp.concatenate(
        [jnp.where(yl == 0, act_in, act_in_other), jnp.where(yl == 0, act_in_other, act_in)], axis=0
    )
    rows = lax.all_gather(rows, "zh", axis=0, tiled=True)
    copies = jnp.broadcast_to(rows[None], (planes,) + rows.shape)
    rows = lax.all_to_all(copies, PLANE, 0, 0, tiled=True)
    rows = rows.transpose(1, 0, 2).reshape(rows.shape[1], planes * share)
    rows_peer = swap(rows, "c")
    rows_own = jnp.where(yl == core, rows, rows_peer)
    rows_other = jnp.where(yl == core, rows_peer, rows)
    basis_half = jnp.concatenate([mine(grad_basis), swap(theirs(grad_basis), "yl")], axis=1)
    basis_peer = swap(basis_half, "c")
    basis_a = jnp.where(yl == core, basis_half, basis_peer)
    basis_b = jnp.where(yl == core, basis_peer, basis_half)

    own_basis = gathered[:, :basis_rows, :cols].reshape(nz * basis_rows, cols)
    other_basis = gathered[:, :basis_rows, cols:].reshape(nz * basis_rows, cols)
    act_proj = (dot(rows_own, own_basis) + dot(rows_other, other_basis)).astype(BF16)
    got_a = gathered[:, basis_rows : basis_rows + capacity].reshape(nz * capacity, hidden)
    got_b = gathered[:, basis_rows + capacity :].reshape(nz * capacity, hidden)
    act_all = lax.all_gather(act_proj, "zl", axis=0, tiled=False)

    part = dot(got_a, basis_a) + dot(got_b, basis_b)
    parts = lax.all_to_all(part.reshape(planes, part.shape[0] // planes, -1), PLANE, 0, 0, tiled=True)
    grad_sq = jnp.square(jnp.sum(parts, axis=0)).astype(BF16)
    copies = jnp.broadcast_to(grad_sq[None], (planes,) + grad_sq.shape)
    grad_sq = lax.all_to_all(copies, PLANE, 0, 0, tiled=True).reshape(nz * capacity, -1)
    grad_sq_other = swap(grad_sq, "c")

    act_sq = jnp.square(act_all.astype(F32)).astype(BF16)
    act_sq = act_sq.reshape(nl, nz // nl, 2, capacity, cols).transpose(2, 1, 0, 3, 4)
    act_sq = act_sq.reshape(2, nz * capacity, cols)
    act_first = lax.dynamic_index_in_dim(act_sq, core, 0, keepdims=False)
    act_second = lax.dynamic_index_in_dim(act_sq, 1 - core, 0, keepdims=False)

    def outer(g, a):
        return lax.dot_general(g, a, (((0,), (0,)), ((), ())), preferred_element_type=F32)

    def block(lo, hi):
        own, other = grad_sq[:, lo:hi], grad_sq_other[:, lo:hi]
        return (outer(own, act_first) + outer(other, act_second)) / token_total

    keys = grad_sq.shape[1]
    got = swap(block(keys // 2, keys), "yl")
    kept = block(0, keys // 2)
    return jnp.stack([jnp.where(yl == 0, kept, got), jnp.where(yl == 0, got, kept)])


def solution(mesh):
    dp, owner = mesh.devices.shape
    split = Mesh(
        mesh.devices.reshape(2, dp // 8, 4, 2, owner // 4, 2), ("yl", "zh", "zl", "yh", "x", "c")
    )
    rows, cols = ("yl", "zh", "zl"), ("yh", "x", "c")
    placed = (
        P(rows, None),
        P(None, rows, cols),
        P(None, cols, rows),
        P(None, rows, cols),
        P(rows, None),
    )
    return jax.shard_map(
        per_device, mesh=split, in_specs=placed, out_specs=P(None, rows, cols), check_vma=False
    )
```

```python
import jax
import jax.numpy as jnp
from jax import lax
from jax.experimental import pallas as pl
from jax.experimental.pallas import tpu as pltpu
from jax.sharding import Mesh, PartitionSpec as P

F32, BF16 = jnp.float32, jnp.bfloat16
PLANE = ("yh", "x")


def choosers(expert_ids, experts, capacity):
    slot_order = jnp.arange(capacity, dtype=jnp.int32)[:, None]
    rows = expert_ids.shape[0]
    before = jnp.tril(jnp.ones((rows, rows), BF16))
    out = []
    for expert in range(experts):
        routed = jnp.any(expert_ids == expert, axis=1)
        count = jnp.dot(before, routed.astype(BF16)[:, None], preferred_element_type=F32)[:, 0]
        slot_index = count.astype(jnp.int32) - 1
        chosen = jnp.logical_and(routed[None, :], slot_index[None, :] == slot_order)
        out.append(chosen.astype(BF16))
    return out


def pick(chooser, rows):
    return jnp.dot(chooser, rows, preferred_element_type=F32).astype(BF16)


def swap(x, axis):
    return lax.ppermute(x, axis, [(0, 1), (1, 0)])


def dot(a, b):
    return jnp.dot(a, b, preferred_element_type=F32)


def project_kernel(got, rows, rows_peer, basis, basis_peer, part, act, total):
    step = pl.program_id(0)
    blocks, height, _ = got.shape
    cols = act.shape[1]
    deep, slots = height // 2, height // 4

    @pl.when(step == 0)
    def _():
        total[...] = jnp.zeros_like(total)

    own = got[:, :deep, :cols].reshape(blocks * deep, cols)
    other = got[:, :deep, cols:].reshape(blocks * deep, cols)
    total[...] += dot(rows[...], own) + dot(rows_peer[...], other)
    grad = got[:, deep : deep + slots].reshape(blocks * slots, 2 * cols)
    grad_peer = got[:, deep + slots :].reshape(blocks * slots, 2 * cols)
    part[...] = (dot(grad, basis[...]) + dot(grad_peer, basis_peer[...])).astype(part.dtype)

    @pl.when(step == pl.num_programs(0) - 1)
    def _():
        act[...] = total[...].astype(act.dtype)


def project(got, rows, rows_peer, basis, basis_peer, blocks):
    nz, height, lanes = got.shape
    count, keys, cols = rows.shape[0], basis.shape[1], lanes // 2
    row_block = pl.BlockSpec((count, blocks * height // 2), lambda i: (0, i))
    whole = pl.BlockSpec(basis.shape, lambda i: (0, 0))
    made = nz * height // 4
    return pl.pallas_call(
        project_kernel,
        grid=(nz // blocks,),
        in_specs=[
            pl.BlockSpec((blocks, height, lanes), lambda i: (i, 0, 0)),
            row_block,
            row_block,
            whole,
            whole,
        ],
        out_specs=[
            pl.BlockSpec((blocks * height // 4, keys), lambda i: (i, 0)),
            pl.BlockSpec((count, cols), lambda i: (0, 0)),
        ],
        out_shape=[
            jax.ShapeDtypeStruct((made, keys), BF16),
            jax.ShapeDtypeStruct((count, cols), BF16),
        ],
        scratch_shapes=[pltpu.VMEM((count, cols), F32)],
        compiler_params=pltpu.CompilerParams(vmem_limit_bytes=32 * 1024 * 1024),
        cost_estimate=pl.CostEstimate(
            flops=4 * made * basis.shape[0] * keys + 4 * count * rows.shape[1] * cols,
            bytes_accessed=2 * (got.size + 2 * rows.size + 2 * basis.size + made * keys + count * cols),
            transcendentals=0,
        ),
    )(got, rows, rows_peer, basis, basis_peer)


def per_device(tokens, act_basis, grad_basis, grads, expert_ids):
    tok_rows, width = tokens.shape
    capacity = tok_rows // 2
    nl = lax.axis_size("zl")
    nz = lax.axis_size("zh") * nl
    token_total = tok_rows * lax.axis_size("yl") * nz
    planes = lax.axis_size("yh") * lax.axis_size("x")
    yl, core = lax.axis_index("yl"), lax.axis_index("c")
    cols = act_basis.shape[2]

    def mine(x):
        return lax.dynamic_index_in_dim(x, yl, 0, keepdims=False)

    def theirs(x):
        return lax.dynamic_index_in_dim(x, 1 - yl, 0, keepdims=False)

    act_other = swap(theirs(act_basis), "yl")
    choose = choosers(expert_ids, 2, capacity)
    picked_grad = jnp.stack([pick(choose[e], grads[e]) for e in range(2)])
    straight = [(2 * y + c, 2 * c + y) for y in range(2) for c in range(2)]
    crossed = [(2 * y + c, 2 * (1 - c) + y) for y in range(2) for c in range(2)]
    grad_a = lax.ppermute(
        lax.dynamic_index_in_dim(picked_grad, core, 0, keepdims=False), ("yl", "c"), straight
    )
    grad_b = lax.ppermute(
        lax.dynamic_index_in_dim(picked_grad, 1 - core, 0, keepdims=False), ("yl", "c"), crossed
    )
    same, act_own = yl == core, mine(act_basis)
    act_rows = jnp.concatenate(
        [jnp.where(same, act_own, act_other), jnp.where(same, act_other, act_own)], axis=1
    )
    payload = jnp.concatenate(
        [act_rows, jnp.where(same, grad_a, grad_b), jnp.where(same, grad_b, grad_a)], axis=0
    )
    gathered = lax.all_gather(payload, ("zh", "zl"), axis=0, tiled=False)

    plane = lax.axis_index("yh") * lax.axis_size("x") + lax.axis_index("x")
    share = width // (2 * planes)
    piece = lax.dynamic_slice_in_dim(tokens, core * (width // 2) + plane * share, share, 1)
    picked_act = jnp.stack([pick(choose[e], piece) for e in range(2)])
    act_in, act_in_other = mine(picked_act), swap(theirs(picked_act), "yl")
    rows = jnp.concatenate(
        [jnp.where(yl == 0, act_in, act_in_other), jnp.where(yl == 0, act_in_other, act_in)], axis=0
    )
    rows = lax.all_gather(rows, "zh", axis=0, tiled=True)
    copies = jnp.broadcast_to(rows[None], (planes,) + rows.shape)
    rows = lax.all_to_all(copies, PLANE, 0, 0, tiled=True)
    rows = rows.transpose(1, 0, 2).reshape(rows.shape[1], planes * share)
    rows_peer = swap(rows, "c")
    basis_half = jnp.concatenate([mine(grad_basis), swap(theirs(grad_basis), "yl")], axis=1)
    basis_peer = swap(basis_half, "c")

    part, act_proj = project(gathered, rows, rows_peer, basis_half, basis_peer, nl)
    act_all = lax.all_gather(act_proj, "zl", axis=0, tiled=False)

    parts = lax.all_to_all(part.reshape(planes, part.shape[0] // planes, -1), PLANE, 0, 0, tiled=True)
    grad_sq = jnp.square(jnp.sum(parts.astype(F32), axis=0)).astype(BF16)
    copies = jnp.broadcast_to(grad_sq[None], (planes,) + grad_sq.shape)
    grad_sq = lax.all_to_all(copies, PLANE, 0, 0, tiled=True).reshape(nz * capacity, -1)
    grad_sq_other = swap(grad_sq, "c")

    act_sq = jnp.square(act_all.astype(F32)).astype(BF16)
    act_sq = act_sq.reshape(nl, nz // nl, 2, capacity, cols).transpose(2, 1, 0, 3, 4)
    act_sq = act_sq.reshape(2, nz * capacity, cols)
    act_first = lax.dynamic_index_in_dim(act_sq, core, 0, keepdims=False)
    act_second = lax.dynamic_index_in_dim(act_sq, 1 - core, 0, keepdims=False)

    def outer(g, a):
        return lax.dot_general(g, a, (((0,), (0,)), ((), ())), preferred_element_type=F32)

    def block(lo, hi):
        own, other = grad_sq[:, lo:hi], grad_sq_other[:, lo:hi]
        return (outer(own, act_first) + outer(other, act_second)) / token_total

    keys = grad_sq.shape[1]
    got = swap(block(keys // 2, keys), "yl")
    kept = block(0, keys // 2)
    return jnp.stack([jnp.where(yl == 0, kept, got), jnp.where(yl == 0, got, kept)])


def solution(mesh):
    dp, owner = mesh.devices.shape
    split = Mesh(
        mesh.devices.reshape(2, dp // 8, 4, 2, owner // 4, 2), ("yl", "zh", "zl", "yh", "x", "c")
    )
    rows, cols = ("yl", "zh", "zl"), ("yh", "x", "c")
    placed = (
        P(rows, None),
        P(None, rows, cols),
        P(None, cols, rows),
        P(None, rows, cols),
        P(rows, None),
    )
    return jax.shard_map(
        per_device, mesh=split, in_specs=placed, out_specs=P(None, rows, cols), check_vma=False
    )
```

```python
import jax
import jax.numpy as jnp
from jax import lax
from jax.experimental import pallas as pl
from jax.experimental.pallas import tpu as pltpu
from jax.sharding import Mesh, PartitionSpec as P

F32, BF16 = jnp.float32, jnp.bfloat16
PLANE = ("yh", "x")


def choosers(expert_ids, experts, capacity):
    slot_order = jnp.arange(capacity, dtype=jnp.int32)[:, None]
    rows = expert_ids.shape[0]
    before = jnp.tril(jnp.ones((rows, rows), BF16))
    out = []
    for expert in range(experts):
        routed = jnp.any(expert_ids == expert, axis=1)
        count = jnp.dot(before, routed.astype(BF16)[:, None], preferred_element_type=F32)[:, 0]
        slot_index = count.astype(jnp.int32) - 1
        chosen = jnp.logical_and(routed[None, :], slot_index[None, :] == slot_order)
        out.append(chosen.astype(BF16))
    return out


def pick(chooser, rows):
    return jnp.dot(chooser, rows, preferred_element_type=F32).astype(BF16)


def swap(x, axis):
    return lax.ppermute(x, axis, [(0, 1), (1, 0)])


def dot(a, b):
    return jnp.dot(a, b, preferred_element_type=F32)


def project_kernel(got, rows, rows_peer, basis, basis_peer, part, act, total):
    step = pl.program_id(0)
    blocks, height, _ = got.shape
    cols = act.shape[1]
    deep, slots = height // 2, height // 4

    @pl.when(step == 0)
    def _():
        total[...] = jnp.zeros_like(total)

    own = got[:, :deep, :cols].reshape(blocks * deep, cols)
    other = got[:, :deep, cols:].reshape(blocks * deep, cols)
    total[...] += dot(rows[...], own) + dot(rows_peer[...], other)
    grad = got[:, deep : deep + slots].reshape(blocks * slots, 2 * cols)
    grad_peer = got[:, deep + slots :].reshape(blocks * slots, 2 * cols)
    sums = dot(grad, basis[...]) + dot(grad_peer, basis_peer[...])
    part[...] = sums.astype(part.dtype).reshape(part.shape)

    @pl.when(step == pl.num_programs(0) - 1)
    def _():
        rounded = total[...].astype(act.dtype).astype(F32)
        act[...] = (rounded * rounded).astype(act.dtype)


def project(got, rows, rows_peer, basis, basis_peer, blocks):
    nz, height, lanes = got.shape
    count, keys, cols = rows.shape[0], basis.shape[1], lanes // 2
    row_block = pl.BlockSpec((count, blocks * height // 2), lambda i: (0, i))
    whole = pl.BlockSpec(basis.shape, lambda i: (0, 0))
    made = nz * height // 4
    return pl.pallas_call(
        project_kernel,
        grid=(nz // blocks,),
        in_specs=[
            pl.BlockSpec((blocks, height, lanes), lambda i: (i, 0, 0)),
            row_block,
            row_block,
            whole,
            whole,
        ],
        out_specs=[
            pl.BlockSpec((blocks, 1, height // 4, keys), lambda i: (0, i, 0, 0)),
            pl.BlockSpec((count, cols), lambda i: (0, 0)),
        ],
        out_shape=[
            jax.ShapeDtypeStruct((blocks, nz // blocks, height // 4, keys), BF16),
            jax.ShapeDtypeStruct((count, cols), BF16),
        ],
        scratch_shapes=[pltpu.VMEM((count, cols), F32)],
        compiler_params=pltpu.CompilerParams(vmem_limit_bytes=56 * 1024 * 1024),
        cost_estimate=pl.CostEstimate(
            flops=4 * made * basis.shape[0] * keys + 4 * count * rows.shape[1] * cols,
            bytes_accessed=2 * (got.size + 2 * rows.size + 2 * basis.size + made * keys + count * cols),
            transcendentals=0,
        ),
    )(got, rows, rows_peer, basis, basis_peer)


def per_device(tokens, act_basis, grad_basis, grads, expert_ids):
    tok_rows, width = tokens.shape
    capacity = tok_rows // 2
    nl = lax.axis_size("zl")
    nz = lax.axis_size("zh") * nl
    token_total = tok_rows * lax.axis_size("yl") * nz
    planes = lax.axis_size("yh") * lax.axis_size("x")
    yl, core = lax.axis_index("yl"), lax.axis_index("c")
    cols = act_basis.shape[2]

    def mine(x):
        return lax.dynamic_index_in_dim(x, yl, 0, keepdims=False)

    def theirs(x):
        return lax.dynamic_index_in_dim(x, 1 - yl, 0, keepdims=False)

    act_other = swap(theirs(act_basis), "yl")
    choose = choosers(expert_ids, 2, capacity)
    picked_grad = jnp.stack([pick(choose[e], grads[e]) for e in range(2)])
    straight = [(2 * y + c, 2 * c + y) for y in range(2) for c in range(2)]
    crossed = [(2 * y + c, 2 * (1 - c) + y) for y in range(2) for c in range(2)]
    grad_a = lax.ppermute(
        lax.dynamic_index_in_dim(picked_grad, core, 0, keepdims=False), ("yl", "c"), straight
    )
    grad_b = lax.ppermute(
        lax.dynamic_index_in_dim(picked_grad, 1 - core, 0, keepdims=False), ("yl", "c"), crossed
    )
    same, act_own = yl == core, mine(act_basis)
    act_rows = jnp.concatenate(
        [jnp.where(same, act_own, act_other), jnp.where(same, act_other, act_own)], axis=1
    )
    payload = jnp.concatenate(
        [act_rows, jnp.where(same, grad_a, grad_b), jnp.where(same, grad_b, grad_a)], axis=0
    )
    gathered = lax.all_gather(payload, ("zh", "zl"), axis=0, tiled=False)

    plane = lax.axis_index("yh") * lax.axis_size("x") + lax.axis_index("x")
    share = width // (2 * planes)
    piece = lax.dynamic_slice_in_dim(tokens, core * (width // 2) + plane * share, share, 1)
    picked_act = jnp.stack([pick(choose[e], piece) for e in range(2)])
    act_in, act_in_other = mine(picked_act), swap(theirs(picked_act), "yl")
    rows = jnp.concatenate(
        [jnp.where(yl == 0, act_in, act_in_other), jnp.where(yl == 0, act_in_other, act_in)], axis=0
    )
    rows = lax.all_gather(rows, "zh", axis=0, tiled=True)
    copies = jnp.broadcast_to(rows[None], (planes,) + rows.shape)
    rows = lax.all_to_all(copies, PLANE, 0, 0, tiled=True)
    rows = rows.reshape(planes, nz // nl, 2, capacity, share).transpose(2, 1, 3, 0, 4)
    rows = rows.reshape(2 * nz // nl * capacity, planes * share)
    rows_peer = swap(rows, "c")
    basis_half = jnp.concatenate([mine(grad_basis), swap(theirs(grad_basis), "yl")], axis=1)
    basis_peer = swap(basis_half, "c")

    part, act_sq = project(gathered, rows, rows_peer, basis_half, basis_peer, nl)
    act_sq = lax.all_gather(act_sq, "zl", axis=0, tiled=False)

    parts = lax.all_to_all(part.reshape(planes, nz * capacity // planes, -1), PLANE, 0, 0, tiled=True)
    grad_sq = jnp.square(jnp.sum(parts.astype(F32), axis=0)).astype(BF16)
    copies = jnp.broadcast_to(grad_sq[None], (planes,) + grad_sq.shape)
    grad_sq = lax.all_to_all(copies, PLANE, 0, 0, tiled=True).reshape(nz * capacity, -1)
    grad_sq_other = swap(grad_sq, "c")

    act_sq = act_sq.reshape(nl, 2, nz // nl * capacity, cols)

    def group(index):
        return lax.dynamic_index_in_dim(act_sq, index, 1, keepdims=False).reshape(nz * capacity, cols)

    act_first, act_second = group(core), group(1 - core)

    def outer(g, a):
        return lax.dot_general(g, a, (((0,), (0,)), ((), ())), preferred_element_type=F32)

    def block(lo, hi):
        own, other = grad_sq[:, lo:hi], grad_sq_other[:, lo:hi]
        return (outer(own, act_first) + outer(other, act_second)) / token_total

    keys = grad_sq.shape[1]
    got = swap(block(keys // 2, keys), "yl")
    kept = block(0, keys // 2)
    return jnp.stack([jnp.where(yl == 0, kept, got), jnp.where(yl == 0, got, kept)])


def solution(mesh):
    dp, owner = mesh.devices.shape
    split = Mesh(
        mesh.devices.reshape(2, dp // 8, 4, 2, owner // 4, 2), ("yl", "zh", "zl", "yh", "x", "c")
    )
    rows, cols = ("yl", "zh", "zl"), ("yh", "x", "c")
    placed = (
        P(rows, None),
        P(None, rows, cols),
        P(None, cols, rows),
        P(None, rows, cols),
        P(rows, None),
    )
    return jax.shard_map(
        per_device, mesh=split, in_specs=placed, out_specs=P(None, rows, cols), check_vma=False
    )
```

```python
import jax
import jax.numpy as jnp
from jax import lax
from jax.experimental import pallas as pl
from jax.experimental.pallas import tpu as pltpu
from jax.sharding import Mesh, PartitionSpec as P

F32, BF16 = jnp.float32, jnp.bfloat16
PLANE = ("yh", "x")


def pick_kernel(ids, grads, picked, chooser):
    experts, capacity, rows = chooser.shape
    first, second = ids[0:1, :], ids[1:2, :]
    source = lax.broadcasted_iota(jnp.int32, (rows, rows), 0)
    target = lax.broadcasted_iota(jnp.int32, (rows, rows), 1)
    before = (source <= target).astype(F32).astype(BF16)
    slot_order = lax.broadcasted_iota(jnp.int32, (capacity, rows), 0)
    for expert in range(experts):
        routed = jnp.logical_or(first == expert, second == expert)
        flags = jnp.broadcast_to(routed.astype(F32), (16, rows)).astype(BF16)
        slot_index = dot(flags, before)[0:1].astype(jnp.int32) - 1
        hit = jnp.logical_and(slot_order == slot_index, routed)
        chosen = hit.astype(F32).astype(BF16)
        chooser[expert] = chosen
        picked[expert] = dot(chosen, grads[expert]).astype(BF16)


def pick_grads(ids, grads, capacity):
    experts, rows, hidden = grads.shape
    return pl.pallas_call(
        pick_kernel,
        out_shape=[
            jax.ShapeDtypeStruct((experts, capacity, hidden), BF16),
            jax.ShapeDtypeStruct((experts, capacity, rows), BF16),
        ],
    )(ids.T, grads)


def swap(x, axis):
    return lax.ppermute(x, axis, [(0, 1), (1, 0)])


def dot(a, b):
    return jnp.dot(a, b, preferred_element_type=F32)


def part_kernel(got, basis, basis_peer, part):
    blocks, height, lanes = got.shape
    slots = height // 2
    own = got[:, :slots].reshape(blocks * slots, lanes)
    other = got[:, slots:].reshape(blocks * slots, lanes)
    sums = dot(own, basis[...]) + dot(other, basis_peer[...])
    part[...] = sums.astype(part.dtype).reshape(part.shape)


def act_kernel(got, rows, rows_peer, act, total):
    step = pl.program_id(0)
    blocks, height, _ = got.shape
    cols = act.shape[1]

    @pl.when(step == 0)
    def _():
        total[...] = jnp.zeros_like(total)

    own = got[:, :, :cols].reshape(blocks * height, cols)
    other = got[:, :, cols:].reshape(blocks * height, cols)
    total[...] += dot(rows[...], own) + dot(rows_peer[...], other)

    @pl.when(step == pl.num_programs(0) - 1)
    def _():
        rounded = total[...].astype(act.dtype).astype(F32)
        act[...] = (rounded * rounded).astype(act.dtype)


ROOM = pltpu.CompilerParams(vmem_limit_bytes=56 * 1024 * 1024)


def partial_sums(got, basis, basis_peer, blocks):
    nz, height, lanes = got.shape
    keys, made = basis.shape[1], height // 4
    whole = pl.BlockSpec(basis.shape, lambda i: (0, 0))
    return pl.pallas_call(
        part_kernel,
        grid=(nz // blocks,),
        in_specs=[pl.BlockSpec((blocks, height // 2, lanes), lambda i: (i, 1, 0)), whole, whole],
        out_specs=pl.BlockSpec((blocks, 1, made, keys), lambda i: (0, i, 0, 0)),
        out_shape=jax.ShapeDtypeStruct((blocks, nz // blocks, made, keys), BF16),
        compiler_params=ROOM,
        cost_estimate=pl.CostEstimate(
            flops=4 * nz * made * lanes * keys,
            bytes_accessed=got.size + 4 * basis.size + 2 * nz * made * keys,
            transcendentals=0,
        ),
    )(got, basis, basis_peer)


def project_act(got, rows, rows_peer, blocks):
    nz, height, lanes = got.shape
    count, cols = rows.shape[0], lanes // 2
    row_block = pl.BlockSpec((count, blocks * height // 2), lambda i: (0, i))
    return pl.pallas_call(
        act_kernel,
        grid=(nz // blocks,),
        in_specs=[
            pl.BlockSpec((blocks, height // 2, lanes), lambda i: (i, 0, 0)),
            row_block,
            row_block,
        ],
        out_specs=pl.BlockSpec((count, cols), lambda i: (0, 0)),
        out_shape=jax.ShapeDtypeStruct((count, cols), BF16),
        scratch_shapes=[pltpu.VMEM((count, cols), F32)],
        compiler_params=ROOM,
        cost_estimate=pl.CostEstimate(
            flops=4 * count * rows.shape[1] * cols,
            bytes_accessed=got.size + 4 * rows.size + 2 * count * cols,
            transcendentals=0,
        ),
    )(got, rows, rows_peer)


def per_device(tokens, act_basis, grad_basis, grads, expert_ids):
    tok_rows, width = tokens.shape
    capacity = tok_rows // 2
    nl = lax.axis_size("zl")
    nz = lax.axis_size("zh") * nl
    token_total = tok_rows * lax.axis_size("yl") * nz
    planes = lax.axis_size("yh") * lax.axis_size("x")
    yl, core = lax.axis_index("yl"), lax.axis_index("c")
    cols = act_basis.shape[2]

    def mine(x):
        return lax.dynamic_index_in_dim(x, yl, 0, keepdims=False)

    def theirs(x):
        return lax.dynamic_index_in_dim(x, 1 - yl, 0, keepdims=False)

    act_other = swap(theirs(act_basis), "yl")
    picked_grad, choose = pick_grads(expert_ids, grads, capacity)
    straight = [(2 * y + c, 2 * c + y) for y in range(2) for c in range(2)]
    crossed = [(2 * y + c, 2 * (1 - c) + y) for y in range(2) for c in range(2)]
    grad_a = lax.ppermute(
        lax.dynamic_index_in_dim(picked_grad, core, 0, keepdims=False), ("yl", "c"), straight
    )
    grad_b = lax.ppermute(
        lax.dynamic_index_in_dim(picked_grad, 1 - core, 0, keepdims=False), ("yl", "c"), crossed
    )
    same, act_own = yl == core, mine(act_basis)
    act_rows = jnp.concatenate(
        [jnp.where(same, act_own, act_other), jnp.where(same, act_other, act_own)], axis=1
    )
    payload = jnp.concatenate(
        [act_rows, jnp.where(same, grad_a, grad_b), jnp.where(same, grad_b, grad_a)], axis=0
    )
    gathered = lax.all_gather(payload, ("zh", "zl"), axis=0, tiled=False)

    plane = lax.axis_index("yh") * lax.axis_size("x") + lax.axis_index("x")
    share = width // (2 * planes)
    piece = lax.dynamic_slice_in_dim(tokens, core * (width // 2) + plane * share, share, 1)
    picked_act = jnp.stack([dot(choose[e], piece).astype(BF16) for e in range(2)])
    act_in, act_in_other = mine(picked_act), swap(theirs(picked_act), "yl")
    rows = jnp.concatenate(
        [jnp.where(yl == 0, act_in, act_in_other), jnp.where(yl == 0, act_in_other, act_in)], axis=0
    )
    rows = lax.all_gather(rows, "zh", axis=0, tiled=True)
    basis_half = jnp.concatenate([mine(grad_basis), swap(theirs(grad_basis), "yl")], axis=1)
    rows, basis_half = lax.optimization_barrier((rows, basis_half))
    basis_peer = swap(basis_half, "c")
    copies = jnp.broadcast_to(rows[None], (planes,) + rows.shape)
    rows = lax.all_to_all(copies, PLANE, 0, 0, tiled=True)
    rows = rows.reshape(planes, nz // nl, 2, capacity, share).transpose(2, 1, 3, 0, 4)
    rows = rows.reshape(2 * nz // nl * capacity, planes * share)
    rows_peer = swap(rows, "c")

    part = partial_sums(gathered, basis_half, basis_peer, nl)
    act_sq = lax.all_gather(project_act(gathered, rows, rows_peer, nl), "zl", axis=0, tiled=False)

    parts = lax.all_to_all(part.reshape(planes, nz * capacity // planes, -1), PLANE, 0, 0, tiled=True)
    grad_sq = jnp.square(jnp.sum(parts.astype(F32), axis=0)).astype(BF16)
    copies = jnp.broadcast_to(grad_sq[None], (planes,) + grad_sq.shape)
    grad_sq = lax.all_to_all(copies, PLANE, 0, 0, tiled=True).reshape(nz * capacity, -1)
    grad_sq_other = swap(grad_sq, "c")

    act_sq = act_sq.reshape(nl, 2, nz // nl * capacity, cols)

    def group(index):
        return lax.dynamic_index_in_dim(act_sq, index, 1, keepdims=False).reshape(nz * capacity, cols)

    act_first, act_second = group(core), group(1 - core)

    def outer(g, a):
        return lax.dot_general(g, a, (((0,), (0,)), ((), ())), preferred_element_type=F32)

    def block(lo, hi):
        own, other = grad_sq[:, lo:hi], grad_sq_other[:, lo:hi]
        return (outer(own, act_first) + outer(other, act_second)) / token_total

    keys = grad_sq.shape[1]
    got = swap(block(keys // 2, keys), "yl")
    kept = block(0, keys // 2)
    expert = lax.broadcasted_iota(jnp.int32, (2,) + kept.shape, 0)
    return jnp.where(expert == yl, kept[None], got[None])


def solution(mesh):
    dp, owner = mesh.devices.shape
    split = Mesh(
        mesh.devices.reshape(2, dp // 8, 4, 2, owner // 4, 2), ("yl", "zh", "zl", "yh", "x", "c")
    )
    rows, cols = ("yl", "zh", "zl"), ("yh", "x", "c")
    placed = (
        P(rows, None),
        P(None, rows, cols),
        P(None, cols, rows),
        P(None, rows, cols),
        P(rows, None),
    )
    return jax.shard_map(
        per_device, mesh=split, in_specs=placed, out_specs=P(None, rows, cols), check_vma=False
    )
```

```python
import jax
import jax.numpy as jnp
from jax import lax
from jax.experimental import pallas as pl
from jax.experimental.pallas import tpu as pltpu
from jax.sharding import Mesh, PartitionSpec as P

F32, BF16 = jnp.float32, jnp.bfloat16
PLANE = ("yh", "x")
VMEM_GRANT = 56


def pick_kernel(ids, grads, picked, chooser):
    experts, capacity, rows = chooser.shape
    first, second = ids[0:1, :], ids[1:2, :]
    source = lax.broadcasted_iota(jnp.int32, (rows, rows), 0)
    target = lax.broadcasted_iota(jnp.int32, (rows, rows), 1)
    before = (source <= target).astype(F32).astype(BF16)
    slot_order = lax.broadcasted_iota(jnp.int32, (capacity, rows), 0)
    for expert in range(experts):
        routed = jnp.logical_or(first == expert, second == expert)
        flags = jnp.broadcast_to(routed.astype(F32), (16, rows)).astype(BF16)
        slot_index = dot(flags, before)[0:1].astype(jnp.int32) - 1
        hit = jnp.logical_and(slot_order == slot_index, routed)
        chosen = hit.astype(F32).astype(BF16)
        chooser[expert] = chosen
        picked[expert] = dot(chosen, grads[expert]).astype(BF16)


def pick_grads(ids, grads, capacity):
    experts, rows, hidden = grads.shape
    return pl.pallas_call(
        pick_kernel,
        out_shape=[
            jax.ShapeDtypeStruct((experts, capacity, hidden), BF16),
            jax.ShapeDtypeStruct((experts, capacity, rows), BF16),
        ],
    )(ids.T, grads)


def swap(x, axis):
    return lax.ppermute(x, axis, [(0, 1), (1, 0)])


def dot(a, b):
    return jnp.dot(a, b, preferred_element_type=F32)


def project_kernel(got, rows, rows_peer, basis, basis_peer, part, act, total):
    step = pl.program_id(0)
    blocks, height, _ = got.shape
    cols = act.shape[1]
    deep, slots = height // 2, height // 4

    @pl.when(step == 0)
    def _():
        total[...] = jnp.zeros_like(total)

    grad = got[:, deep : deep + slots].reshape(blocks * slots, 2 * cols)
    grad_peer = got[:, deep + slots :].reshape(blocks * slots, 2 * cols)
    sums = dot(grad, basis[...]) + dot(grad_peer, basis_peer[...])
    part[...] = sums.astype(part.dtype).reshape(part.shape)
    own = got[:, :deep, :cols].reshape(blocks * deep, cols)
    other = got[:, :deep, cols:].reshape(blocks * deep, cols)
    total[...] += dot(rows[...], own) + dot(rows_peer[...], other)

    @pl.when(step == pl.num_programs(0) - 1)
    def _():
        rounded = total[...].astype(act.dtype).astype(F32)
        act[...] = (rounded * rounded).astype(act.dtype)


def project(got, rows, rows_peer, basis, basis_peer, blocks):
    nz, height, lanes = got.shape
    count, keys, cols = rows.shape[0], basis.shape[1], lanes // 2
    row_block = pl.BlockSpec((count, blocks * height // 2), lambda i: (0, i))
    whole = pl.BlockSpec(basis.shape, lambda i: (0, 0))
    made = nz * height // 4
    return pl.pallas_call(
        project_kernel,
        grid=(nz // blocks,),
        in_specs=[
            pl.BlockSpec((blocks, height, lanes), lambda i: (i, 0, 0)),
            row_block,
            row_block,
            whole,
            whole,
        ],
        out_specs=[
            pl.BlockSpec((blocks, 1, height // 4, keys), lambda i: (0, i, 0, 0)),
            pl.BlockSpec((count, cols), lambda i: (0, 0)),
        ],
        out_shape=[
            jax.ShapeDtypeStruct((blocks, nz // blocks, height // 4, keys), BF16),
            jax.ShapeDtypeStruct((count, cols), BF16),
        ],
        scratch_shapes=[pltpu.VMEM((count, cols), F32)],
        compiler_params=pltpu.CompilerParams(vmem_limit_bytes=VMEM_GRANT * 1024 * 1024),
        cost_estimate=pl.CostEstimate(
            flops=4 * made * basis.shape[0] * keys + 4 * count * rows.shape[1] * cols,
            bytes_accessed=2 * (got.size + 2 * rows.size + 2 * basis.size + made * keys + count * cols),
            transcendentals=0,
        ),
    )(got, rows, rows_peer, basis, basis_peer)


def per_device(tokens, act_basis, grad_basis, grads, expert_ids):
    tok_rows, width = tokens.shape
    capacity = tok_rows // 2
    nl = lax.axis_size("zl")
    nz = lax.axis_size("zh") * nl
    token_total = tok_rows * lax.axis_size("yl") * nz
    planes = lax.axis_size("yh") * lax.axis_size("x")
    yl, core = lax.axis_index("yl"), lax.axis_index("c")
    cols = act_basis.shape[2]

    def mine(x):
        return lax.dynamic_index_in_dim(x, yl, 0, keepdims=False)

    def theirs(x):
        return lax.dynamic_index_in_dim(x, 1 - yl, 0, keepdims=False)

    act_other = swap(theirs(act_basis), "yl")
    picked_grad, choose = pick_grads(expert_ids, grads, capacity)
    straight = [(2 * y + c, 2 * c + y) for y in range(2) for c in range(2)]
    crossed = [(2 * y + c, 2 * (1 - c) + y) for y in range(2) for c in range(2)]
    grad_a = lax.ppermute(
        lax.dynamic_index_in_dim(picked_grad, core, 0, keepdims=False), ("yl", "c"), straight
    )
    grad_b = lax.ppermute(
        lax.dynamic_index_in_dim(picked_grad, 1 - core, 0, keepdims=False), ("yl", "c"), crossed
    )
    same, act_own = yl == core, mine(act_basis)
    act_rows = jnp.concatenate(
        [jnp.where(same, act_own, act_other), jnp.where(same, act_other, act_own)], axis=1
    )
    payload = jnp.concatenate(
        [act_rows, jnp.where(same, grad_a, grad_b), jnp.where(same, grad_b, grad_a)], axis=0
    )
    gathered = lax.all_gather(payload, ("zh", "zl"), axis=0, tiled=False)

    plane = lax.axis_index("yh") * lax.axis_size("x") + lax.axis_index("x")
    share = width // (2 * planes)
    piece = lax.dynamic_slice_in_dim(tokens, core * (width // 2) + plane * share, share, 1)
    picked_act = jnp.stack([dot(choose[e], piece).astype(BF16) for e in range(2)])
    act_in, act_in_other = mine(picked_act), swap(theirs(picked_act), "yl")
    rows = jnp.concatenate(
        [jnp.where(yl == 0, act_in, act_in_other), jnp.where(yl == 0, act_in_other, act_in)], axis=0
    )
    rows = lax.all_gather(rows, "zh", axis=0, tiled=True)
    basis_half = jnp.concatenate([mine(grad_basis), swap(theirs(grad_basis), "yl")], axis=1)
    rows, basis_half = lax.optimization_barrier((rows, basis_half))
    basis_peer = swap(basis_half, "c")
    copies = jnp.broadcast_to(rows[None], (planes,) + rows.shape)
    rows = lax.all_to_all(copies, PLANE, 0, 0, tiled=True)
    rows = rows.reshape(planes, nz // nl, 2, capacity, share).transpose(2, 1, 3, 0, 4)
    rows = rows.reshape(2 * nz // nl * capacity, planes * share)
    rows_peer = swap(rows, "c")

    part, act_sq = project(gathered, rows, rows_peer, basis_half, basis_peer, nl)
    act_sq = lax.all_gather(act_sq, "zl", axis=0, tiled=False)

    parts = lax.fori_loop(
        0,
        lax.optimization_barrier(jnp.int32(1)),
        lambda trip, x: lax.all_to_all(x, PLANE, 0, 0, tiled=True),
        part.reshape(planes, nz * capacity // planes, -1),
    )
    grad_sq = jnp.square(jnp.sum(parts.astype(F32), axis=0)).astype(BF16)
    copies = jnp.broadcast_to(grad_sq[None], (planes,) + grad_sq.shape)
    grad_sq = lax.all_to_all(copies, PLANE, 0, 0, tiled=True).reshape(nz * capacity, -1)
    grad_sq_other = swap(grad_sq, "c")

    act_sq = act_sq.reshape(nl, 2, nz // nl * capacity, cols)

    def group(index):
        return lax.dynamic_index_in_dim(act_sq, index, 1, keepdims=False).reshape(nz * capacity, cols)

    act_first, act_second = group(core), group(1 - core)

    def outer(g, a):
        return lax.dot_general(g, a, (((0,), (0,)), ((), ())), preferred_element_type=F32)

    def block(lo, hi):
        own, other = grad_sq[:, lo:hi], grad_sq_other[:, lo:hi]
        return (outer(own, act_first) + outer(other, act_second)) / token_total

    keys = grad_sq.shape[1]
    got = swap(block(keys // 2, keys), "yl")
    kept = block(0, keys // 2)
    expert = lax.broadcasted_iota(jnp.int32, (2,) + kept.shape, 0)
    return jnp.where(expert == yl, kept[None], got[None])


def solution(mesh):
    dp, owner = mesh.devices.shape
    split = Mesh(
        mesh.devices.reshape(2, dp // 8, 4, 2, owner // 4, 2), ("yl", "zh", "zl", "yh", "x", "c")
    )
    rows, cols = ("yl", "zh", "zl"), ("yh", "x", "c")
    placed = (
        P(rows, None),
        P(None, rows, cols),
        P(None, cols, rows),
        P(None, rows, cols),
        P(rows, None),
    )
    return jax.shard_map(
        per_device, mesh=split, in_specs=placed, out_specs=P(None, rows, cols), check_vma=False
    )
```

```python
import jax
import jax.numpy as jnp
from jax import lax
from jax.experimental import pallas as pl
from jax.experimental.pallas import tpu as pltpu
from jax.sharding import Mesh, PartitionSpec as P

F32, BF16 = jnp.float32, jnp.bfloat16
PLANE = ("yh", "x")
VMEM_GRANT = 24


def pick_kernel(ids, grads, picked, chooser):
    experts, capacity, rows = chooser.shape
    first, second = ids[0:1, :], ids[1:2, :]
    source = lax.broadcasted_iota(jnp.int32, (rows, rows), 0)
    target = lax.broadcasted_iota(jnp.int32, (rows, rows), 1)
    before = (source <= target).astype(F32).astype(BF16)
    slot_order = lax.broadcasted_iota(jnp.int32, (capacity, rows), 0)
    for expert in range(experts):
        routed = jnp.logical_or(first == expert, second == expert)
        flags = jnp.broadcast_to(routed.astype(F32), (16, rows)).astype(BF16)
        slot_index = dot(flags, before)[0:1].astype(jnp.int32) - 1
        hit = jnp.logical_and(slot_order == slot_index, routed)
        chosen = hit.astype(F32).astype(BF16)
        chooser[expert] = chosen
        picked[expert] = dot(chosen, grads[expert]).astype(BF16)


def pick_grads(ids, grads, capacity):
    experts, rows, hidden = grads.shape
    return pl.pallas_call(
        pick_kernel,
        out_shape=[
            jax.ShapeDtypeStruct((experts, capacity, hidden), BF16),
            jax.ShapeDtypeStruct((experts, capacity, rows), BF16),
        ],
    )(ids.T, grads)


def swap(x, axis):
    return lax.ppermute(x, axis, [(0, 1), (1, 0)])


def dot(a, b):
    return jnp.dot(a, b, preferred_element_type=F32)


def project_kernel(got, rows, rows_peer, basis, basis_peer, part, act):
    blocks, steps = part.shape[:2]
    height = got.shape[1]
    cols = act.shape[1]
    deep, slots = height // 2, height // 4
    total = None
    for step in range(steps):
        span = slice(step * blocks, (step + 1) * blocks)
        deeps = slice(step * blocks * deep, (step + 1) * blocks * deep)
        grad = got[span, deep : deep + slots].reshape(blocks * slots, 2 * cols)
        grad_peer = got[span, deep + slots :].reshape(blocks * slots, 2 * cols)
        sums = dot(grad, basis[...]) + dot(grad_peer, basis_peer[...])
        part[:, step] = sums.astype(part.dtype).reshape(blocks, slots, 2 * cols)
        own = got[span, :deep, :cols].reshape(blocks * deep, cols)
        other = got[span, :deep, cols:].reshape(blocks * deep, cols)
        more = dot(rows[:, deeps], own) + dot(rows_peer[:, deeps], other)
        total = more if total is None else total + more
    rounded = total.astype(act.dtype).astype(F32)
    act[...] = (rounded * rounded).astype(act.dtype)


def project(got, rows, rows_peer, basis, basis_peer, blocks):
    nz, height, lanes = got.shape
    count, keys, cols = rows.shape[0], basis.shape[1], lanes // 2
    steps, made = nz // blocks, height // 4
    near = pl.BlockSpec(memory_space=pltpu.VMEM)
    return pl.pallas_call(
        project_kernel,
        in_specs=[near] * 5,
        out_specs=[near] * 2,
        out_shape=[
            jax.ShapeDtypeStruct((blocks, steps, made, keys), BF16),
            jax.ShapeDtypeStruct((count, cols), BF16),
        ],
        compiler_params=pltpu.CompilerParams(vmem_limit_bytes=VMEM_GRANT * 1024 * 1024),
        cost_estimate=pl.CostEstimate(
            flops=4 * nz * made * basis.shape[0] * keys + 4 * count * rows.shape[1] * cols,
            bytes_accessed=2 * (got.size + 2 * rows.size + 2 * basis.size + nz * made * keys + count * cols),
            transcendentals=0,
        ),
    )(got, rows, rows_peer, basis, basis_peer)


def per_device(tokens, act_basis, grad_basis, grads, expert_ids):
    tok_rows, width = tokens.shape
    capacity = tok_rows // 2
    nl = lax.axis_size("zl")
    nz = lax.axis_size("zh") * nl
    token_total = tok_rows * lax.axis_size("yl") * nz
    planes = lax.axis_size("yh") * lax.axis_size("x")
    yl, core = lax.axis_index("yl"), lax.axis_index("c")
    cols = act_basis.shape[2]

    def mine(x):
        return lax.dynamic_index_in_dim(x, yl, 0, keepdims=False)

    def theirs(x):
        return lax.dynamic_index_in_dim(x, 1 - yl, 0, keepdims=False)

    act_other = swap(theirs(act_basis), "yl")
    picked_grad, choose = pick_grads(expert_ids, grads, capacity)
    straight = [(2 * y + c, 2 * c + y) for y in range(2) for c in range(2)]
    crossed = [(2 * y + c, 2 * (1 - c) + y) for y in range(2) for c in range(2)]
    grad_a = lax.ppermute(
        lax.dynamic_index_in_dim(picked_grad, core, 0, keepdims=False), ("yl", "c"), straight
    )
    grad_b = lax.ppermute(
        lax.dynamic_index_in_dim(picked_grad, 1 - core, 0, keepdims=False), ("yl", "c"), crossed
    )
    same, act_own = yl == core, mine(act_basis)
    act_rows = jnp.concatenate(
        [jnp.where(same, act_own, act_other), jnp.where(same, act_other, act_own)], axis=1
    )
    payload = jnp.concatenate(
        [act_rows, jnp.where(same, grad_a, grad_b), jnp.where(same, grad_b, grad_a)], axis=0
    )
    gathered = lax.all_gather(payload, ("zh", "zl"), axis=0, tiled=False)

    plane = lax.axis_index("yh") * lax.axis_size("x") + lax.axis_index("x")
    share = width // (2 * planes)
    piece = lax.dynamic_slice_in_dim(tokens, core * (width // 2) + plane * share, share, 1)
    picked_act = jnp.stack([dot(choose[e], piece).astype(BF16) for e in range(2)])
    act_in, act_in_other = mine(picked_act), swap(theirs(picked_act), "yl")
    rows = jnp.concatenate(
        [jnp.where(yl == 0, act_in, act_in_other), jnp.where(yl == 0, act_in_other, act_in)], axis=0
    )
    rows = lax.all_gather(rows, "zh", axis=0, tiled=True)
    basis_half = jnp.concatenate([mine(grad_basis), swap(theirs(grad_basis), "yl")], axis=1)
    rows, basis_half = lax.optimization_barrier((rows, basis_half))
    basis_peer = swap(basis_half, "c")
    copies = jnp.broadcast_to(rows[None], (planes,) + rows.shape)
    rows = lax.all_to_all(copies, PLANE, 0, 0, tiled=True)
    def lay(x):
        x = x.reshape(planes, nz // nl, 2, capacity, share).transpose(2, 1, 3, 0, 4)
        return x.reshape(2 * nz // nl * capacity, planes * share)

    rows, rows_peer = lay(rows), lay(swap(rows, "c"))

    part, act_sq = project(gathered, rows, rows_peer, basis_half, basis_peer, nl)
    act_sq = lax.all_gather(act_sq, "zl", axis=0, tiled=False)

    parts = lax.cond(
        lax.optimization_barrier(jnp.int32(1)) > 0,
        lambda x: lax.all_to_all(x, PLANE, 0, 0, tiled=True),
        lambda x: x,
        part.reshape(planes, nz * capacity // planes, -1),
    )
    grad_sq = jnp.square(jnp.sum(parts.astype(F32), axis=0)).astype(BF16)
    copies = jnp.broadcast_to(grad_sq[None], (planes,) + grad_sq.shape)
    grad_sq = lax.all_to_all(copies, PLANE, 0, 0, tiled=True).reshape(nz * capacity, -1)
    grad_sq_other = swap(grad_sq, "c")

    act_sq = act_sq.reshape(nl, 2, nz // nl * capacity, cols)

    def group(index):
        return lax.dynamic_index_in_dim(act_sq, index, 1, keepdims=False).reshape(nz * capacity, cols)

    act_first, act_second = group(core), group(1 - core)

    def outer(g, a):
        return lax.dot_general(g, a, (((0,), (0,)), ((), ())), preferred_element_type=F32)

    def block(lo, hi):
        own, other = grad_sq[:, lo:hi], grad_sq_other[:, lo:hi]
        return (outer(own, act_first) + outer(other, act_second)) / token_total

    keys = grad_sq.shape[1]
    got = swap(block(keys // 2, keys), "yl")
    kept = block(0, keys // 2)
    expert = lax.broadcasted_iota(jnp.int32, (2,) + kept.shape, 0)
    return jnp.where(expert == yl, kept[None], got[None])


def solution(mesh):
    dp, owner = mesh.devices.shape
    split = Mesh(
        mesh.devices.reshape(2, dp // 8, 4, 2, owner // 4, 2), ("yl", "zh", "zl", "yh", "x", "c")
    )
    rows, cols = ("yl", "zh", "zl"), ("yh", "x", "c")
    placed = (
        P(rows, None),
        P(None, rows, cols),
        P(None, cols, rows),
        P(None, rows, cols),
        P(rows, None),
    )
    return jax.shard_map(
        per_device, mesh=split, in_specs=placed, out_specs=P(None, rows, cols), check_vma=False
    )
```

```python
import jax
import jax.numpy as jnp
from jax import lax
from jax.experimental import pallas as pl
from jax.experimental.pallas import tpu as pltpu
from jax.sharding import Mesh, PartitionSpec as P

F32, BF16 = jnp.float32, jnp.bfloat16
PLANE = ("yh", "x")
VMEM_GRANT = 56


def pick_kernel(ids, grads, picked, chooser):
    experts, capacity, rows = chooser.shape
    first, second = ids[0:1, :], ids[1:2, :]
    source = lax.broadcasted_iota(jnp.int32, (rows, rows), 0)
    target = lax.broadcasted_iota(jnp.int32, (rows, rows), 1)
    before = (source <= target).astype(F32).astype(BF16)
    slot_order = lax.broadcasted_iota(jnp.int32, (capacity, rows), 0)
    for expert in range(experts):
        routed = jnp.logical_or(first == expert, second == expert)
        flags = jnp.broadcast_to(routed.astype(F32), (16, rows)).astype(BF16)
        slot_index = dot(flags, before)[0:1].astype(jnp.int32) - 1
        hit = jnp.logical_and(slot_order == slot_index, routed)
        chosen = hit.astype(F32).astype(BF16)
        chooser[expert] = chosen
        picked[expert] = dot(chosen, grads[expert]).astype(BF16)


def pick_grads(ids, grads, capacity):
    experts, rows, hidden = grads.shape
    return pl.pallas_call(
        pick_kernel,
        out_shape=[
            jax.ShapeDtypeStruct((experts, capacity, hidden), BF16),
            jax.ShapeDtypeStruct((experts, capacity, rows), BF16),
        ],
    )(ids.T, grads)


def swap(x, axis):
    return lax.ppermute(x, axis, [(0, 1), (1, 0)])


def dot(a, b):
    return jnp.dot(a, b, preferred_element_type=F32)


def project_kernel(got, rows, rows_peer, basis, basis_peer, part, act, total):
    step = pl.program_id(0)
    blocks, height, _ = got.shape
    cols = act.shape[1]
    deep, slots = height // 2, height // 4

    @pl.when(step == 0)
    def _():
        total[...] = jnp.zeros_like(total)

    grad = got[:, deep : deep + slots].reshape(blocks * slots, 2 * cols)
    grad_peer = got[:, deep + slots :].reshape(blocks * slots, 2 * cols)
    sums = dot(grad, basis[...]) + dot(grad_peer, basis_peer[...])
    sums = sums.astype(part.dtype).reshape((part.shape[1], part.shape[0]) + part.shape[2:])
    for group in range(part.shape[1]):
        part[:, group] = sums[group]
    own = got[:, :deep, :cols].reshape(blocks * deep, cols)
    other = got[:, :deep, cols:].reshape(blocks * deep, cols)
    total[...] += dot(rows[...], own) + dot(rows_peer[...], other)

    @pl.when(step == pl.num_programs(0) - 1)
    def _():
        rounded = total[...].astype(act.dtype).astype(F32)
        act[...] = (rounded * rounded).astype(act.dtype)


def project(got, rows, rows_peer, basis, basis_peer, blocks):
    nz, height, lanes = got.shape
    count, keys, cols = rows.shape[0], basis.shape[1], lanes // 2
    row_block = pl.BlockSpec((count, 2 * blocks * height // 2), lambda i: (0, i))
    whole = pl.BlockSpec(basis.shape, lambda i: (0, 0))
    made = nz * height // 4
    groups = 2
    step = groups * blocks
    return pl.pallas_call(
        project_kernel,
        grid=(nz // step,),
        in_specs=[
            pl.BlockSpec((step, height, lanes), lambda i: (i, 0, 0)),
            row_block,
            row_block,
            whole,
            whole,
        ],
        out_specs=[
            pl.BlockSpec((blocks, groups, height // 4, keys), lambda i: (0, i, 0, 0)),
            pl.BlockSpec((count, cols), lambda i: (0, 0)),
        ],
        out_shape=[
            jax.ShapeDtypeStruct((blocks, nz // blocks, height // 4, keys), BF16),
            jax.ShapeDtypeStruct((count, cols), BF16),
        ],
        scratch_shapes=[pltpu.VMEM((count, cols), F32)],
        compiler_params=pltpu.CompilerParams(vmem_limit_bytes=VMEM_GRANT * 1024 * 1024),
        cost_estimate=pl.CostEstimate(
            flops=4 * made * basis.shape[0] * keys + 4 * count * rows.shape[1] * cols,
            bytes_accessed=2 * (got.size + 2 * rows.size + 2 * basis.size + made * keys + count * cols),
            transcendentals=0,
        ),
    )(got, rows, rows_peer, basis, basis_peer)


def per_device(tokens, act_basis, grad_basis, grads, expert_ids):
    tok_rows, width = tokens.shape
    capacity = tok_rows // 2
    nl = lax.axis_size("zl")
    nz = lax.axis_size("zh") * nl
    token_total = tok_rows * lax.axis_size("yl") * nz
    planes = lax.axis_size("yh") * lax.axis_size("x")
    yl, core = lax.axis_index("yl"), lax.axis_index("c")
    cols = act_basis.shape[2]

    def mine(x):
        return lax.dynamic_index_in_dim(x, yl, 0, keepdims=False)

    def theirs(x):
        return lax.dynamic_index_in_dim(x, 1 - yl, 0, keepdims=False)

    act_other = swap(theirs(act_basis), "yl")
    picked_grad, choose = pick_grads(expert_ids, grads, capacity)
    straight = [(2 * y + c, 2 * c + y) for y in range(2) for c in range(2)]
    crossed = [(2 * y + c, 2 * (1 - c) + y) for y in range(2) for c in range(2)]
    grad_a = lax.ppermute(
        lax.dynamic_index_in_dim(picked_grad, core, 0, keepdims=False), ("yl", "c"), straight
    )
    grad_b = lax.ppermute(
        lax.dynamic_index_in_dim(picked_grad, 1 - core, 0, keepdims=False), ("yl", "c"), crossed
    )
    act_rows = jnp.concatenate([mine(act_basis), act_other], axis=1)
    payload = jnp.concatenate([act_rows, grad_a, grad_b], axis=0)
    gathered = lax.all_gather(payload, ("zh", "zl"), axis=0, tiled=False)

    plane = lax.axis_index("yh") * lax.axis_size("x") + lax.axis_index("x")
    share = width // (2 * planes)
    piece = lax.dynamic_slice_in_dim(tokens, core * (width // 2) + plane * share, share, 1)
    picked_act = jnp.stack([dot(choose[e], piece).astype(BF16) for e in range(2)])
    act_in, act_in_other = mine(picked_act), swap(theirs(picked_act), "yl")
    rows = jnp.concatenate(
        [jnp.where(yl == 0, act_in, act_in_other), jnp.where(yl == 0, act_in_other, act_in)], axis=0
    )
    rows = lax.all_gather(rows, "zh", axis=0, tiled=True)
    basis_half = jnp.concatenate([mine(grad_basis), swap(theirs(grad_basis), "yl")], axis=1)
    rows, basis_half = lax.optimization_barrier((rows, basis_half))
    basis_peer = swap(basis_half, "c")
    copies = jnp.broadcast_to(rows[None], (planes,) + rows.shape)
    rows = lax.all_to_all(copies, PLANE, 0, 0, tiled=True)
    rows = rows.reshape(planes, nz // nl, 2, capacity, share).transpose(2, 1, 3, 0, 4)
    rows = rows.reshape(2 * nz // nl * capacity, planes * share)
    rows_peer = swap(rows, "c")

    same = yl == core
    rows_a, rows_b = jnp.where(same, rows, rows_peer), jnp.where(same, rows_peer, rows)
    basis_a = jnp.where(same, basis_half, basis_peer)
    basis_b = jnp.where(same, basis_peer, basis_half)
    part, act_sq = project(gathered, rows_a, rows_b, basis_a, basis_b, nl)
    act_sq = lax.all_gather(act_sq, "zl", axis=0, tiled=False)

    parts = lax.cond(
        lax.optimization_barrier(jnp.int32(1)) > 0,
        lambda x: lax.all_to_all(x, PLANE, 0, 0, tiled=True),
        lambda x: x,
        part.reshape(planes, nz * capacity // planes, -1),
    )
    grad_sq = jnp.square(jnp.sum(parts.astype(F32), axis=0)).astype(BF16)
    copies = jnp.broadcast_to(grad_sq[None], (planes,) + grad_sq.shape)
    grad_sq = lax.all_to_all(copies, PLANE, 0, 0, tiled=True).reshape(nz * capacity, -1)
    grad_sq_other = swap(grad_sq, "c")

    act_sq = act_sq.reshape(nl, 2, nz // nl * capacity, cols)

    def group(index):
        return lax.dynamic_index_in_dim(act_sq, index, 1, keepdims=False).reshape(nz * capacity, cols)

    act_first, act_second = group(core), group(1 - core)

    def outer(g, a):
        return lax.dot_general(g, a, (((0,), (0,)), ((), ())), preferred_element_type=F32)

    def block(lo, hi):
        own, other = grad_sq[:, lo:hi], grad_sq_other[:, lo:hi]
        return (outer(own, act_first) + outer(other, act_second)) / token_total

    keys = grad_sq.shape[1]
    got = swap(block(keys // 2, keys), "yl")
    kept = block(0, keys // 2)
    expert = lax.broadcasted_iota(jnp.int32, (2,) + kept.shape, 0)
    return jnp.where(expert == yl, kept[None], got[None])


def solution(mesh):
    dp, owner = mesh.devices.shape
    split = Mesh(
        mesh.devices.reshape(2, dp // 8, 4, 2, owner // 4, 2), ("yl", "zh", "zl", "yh", "x", "c")
    )
    rows, cols = ("yl", "zh", "zl"), ("yh", "x", "c")
    placed = (
        P(rows, None),
        P(None, rows, cols),
        P(None, cols, rows),
        P(None, rows, cols),
        P(rows, None),
    )
    return jax.shard_map(
        per_device, mesh=split, in_specs=placed, out_specs=P(None, rows, cols), check_vma=False
    )
```

```python
import jax
import jax.numpy as jnp
from jax import lax
from jax.experimental import pallas as pl
from jax.experimental.pallas import tpu as pltpu
from jax.sharding import Mesh, PartitionSpec as P

F32, BF16 = jnp.float32, jnp.bfloat16
PLANE = ("yh", "x")
VMEM_GRANT = 46


def pick_kernel(ids, grads, picked, chooser):
    experts, capacity, rows = chooser.shape
    first, second = ids[0:1, :], ids[1:2, :]
    source = lax.broadcasted_iota(jnp.int32, (rows, rows), 0)
    target = lax.broadcasted_iota(jnp.int32, (rows, rows), 1)
    before = (source <= target).astype(F32).astype(BF16)
    slot_order = lax.broadcasted_iota(jnp.int32, (capacity, rows), 0)
    for expert in range(experts):
        routed = jnp.logical_or(first == expert, second == expert)
        flags = jnp.broadcast_to(routed.astype(F32), (16, rows)).astype(BF16)
        slot_index = dot(flags, before)[0:1].astype(jnp.int32) - 1
        hit = jnp.logical_and(slot_order == slot_index, routed)
        chosen = hit.astype(F32).astype(BF16)
        chooser[expert] = chosen
        picked[expert] = dot(chosen, grads[expert]).astype(BF16)


def pick_grads(ids, grads, capacity):
    experts, rows, hidden = grads.shape
    return pl.pallas_call(
        pick_kernel,
        out_shape=[
            jax.ShapeDtypeStruct((experts, capacity, hidden), BF16),
            jax.ShapeDtypeStruct((experts, capacity, rows), BF16),
        ],
    )(ids.T, grads)


def swap(x, axis):
    return lax.ppermute(x, axis, [(0, 1), (1, 0)])


def dot(a, b):
    return jnp.dot(a, b, preferred_element_type=F32)


def project_kernel(got, rows, rows_peer, basis, basis_peer, part, act, total):
    step = pl.program_id(0)
    blocks, height, _ = got.shape
    cols = act.shape[1]
    deep, slots = height // 2, height // 4

    @pl.when(step == 0)
    def _():
        total[...] = jnp.zeros_like(total)

    grad = got[:, deep : deep + slots].reshape(blocks * slots, 2 * cols)
    grad_peer = got[:, deep + slots :].reshape(blocks * slots, 2 * cols)
    sums = dot(grad, basis[...]) + dot(grad_peer, basis_peer[...])
    sums = sums.astype(part.dtype).reshape((part.shape[1], part.shape[0]) + part.shape[2:])
    for group in range(part.shape[1]):
        part[:, group] = sums[group]
    own = got[:, :deep, :cols].reshape(blocks * deep, cols)
    other = got[:, :deep, cols:].reshape(blocks * deep, cols)
    total[...] += dot(rows[...], own) + dot(rows_peer[...], other)

    @pl.when(step == pl.num_programs(0) - 1)
    def _():
        rounded = total[...].astype(act.dtype).astype(F32)
        act[...] = (rounded * rounded).astype(act.dtype)


def project(got, rows, rows_peer, basis, basis_peer, blocks):
    nz, height, lanes = got.shape
    count, keys, cols = rows.shape[0], basis.shape[1], lanes // 2
    row_block = pl.BlockSpec((count, 2 * blocks * height // 2), lambda i: (0, i))
    whole = pl.BlockSpec(basis.shape, lambda i: (0, 0))
    made = nz * height // 4
    groups = 2
    step = groups * blocks
    return pl.pallas_call(
        project_kernel,
        grid=(nz // step,),
        in_specs=[
            pl.BlockSpec((step, height, lanes), lambda i: (i, 0, 0)),
            row_block,
            row_block,
            whole,
            whole,
        ],
        out_specs=[
            pl.BlockSpec((blocks, groups, height // 4, keys), lambda i: (0, i, 0, 0)),
            pl.BlockSpec((count, cols), lambda i: (0, 0)),
        ],
        out_shape=[
            jax.ShapeDtypeStruct((blocks, nz // blocks, height // 4, keys), BF16),
            jax.ShapeDtypeStruct((count, cols), BF16),
        ],
        scratch_shapes=[pltpu.VMEM((count, cols), F32)],
        compiler_params=pltpu.CompilerParams(vmem_limit_bytes=VMEM_GRANT * 1024 * 1024),
        cost_estimate=pl.CostEstimate(
            flops=4 * made * basis.shape[0] * keys + 4 * count * rows.shape[1] * cols,
            bytes_accessed=2 * (got.size + 2 * rows.size + 2 * basis.size + made * keys + count * cols),
            transcendentals=0,
        ),
    )(got, rows, rows_peer, basis, basis_peer)


def per_device(tokens, act_basis, grad_basis, grads, expert_ids):
    tok_rows, width = tokens.shape
    capacity = tok_rows // 2
    nl = lax.axis_size("zl")
    nz = lax.axis_size("zh") * nl
    token_total = tok_rows * lax.axis_size("yl") * nz
    planes = lax.axis_size("yh") * lax.axis_size("x")
    yl, core = lax.axis_index("yl"), lax.axis_index("c")
    cols = act_basis.shape[2]

    def mine(x):
        return lax.dynamic_index_in_dim(x, yl, 0, keepdims=False)

    def theirs(x):
        return lax.dynamic_index_in_dim(x, 1 - yl, 0, keepdims=False)

    act_other = swap(theirs(act_basis), "yl")
    picked_grad, choose = pick_grads(expert_ids, grads, capacity)
    straight = [(2 * y + c, 2 * c + y) for y in range(2) for c in range(2)]
    crossed = [(2 * y + c, 2 * (1 - c) + y) for y in range(2) for c in range(2)]
    grad_a = lax.ppermute(
        lax.dynamic_index_in_dim(picked_grad, core, 0, keepdims=False), ("yl", "c"), straight
    )
    grad_b = lax.ppermute(
        lax.dynamic_index_in_dim(picked_grad, 1 - core, 0, keepdims=False), ("yl", "c"), crossed
    )
    act_rows = jnp.concatenate([mine(act_basis), act_other], axis=1)
    payload = jnp.concatenate([act_rows, grad_a, grad_b], axis=0)
    gathered = lax.all_gather(payload, ("zh", "zl"), axis=0, tiled=False)

    plane = lax.axis_index("yh") * lax.axis_size("x") + lax.axis_index("x")
    share = width // (2 * planes)
    piece = lax.dynamic_slice_in_dim(tokens, core * (width // 2) + plane * share, share, 1)
    picked_act = jnp.stack([dot(choose[e], piece).astype(BF16) for e in range(2)])
    act_in, act_in_other = mine(picked_act), swap(theirs(picked_act), "yl")
    rows = jnp.concatenate(
        [jnp.where(yl == 0, act_in, act_in_other), jnp.where(yl == 0, act_in_other, act_in)], axis=0
    )
    rows = lax.all_gather(rows, "zh", axis=0, tiled=True)
    basis_half = jnp.concatenate([mine(grad_basis), swap(theirs(grad_basis), "yl")], axis=1)
    rows, basis_half = lax.optimization_barrier((rows, basis_half))
    basis_peer = swap(basis_half, "c")
    copies = jnp.broadcast_to(rows[None], (planes,) + rows.shape)
    rows = lax.all_to_all(copies, PLANE, 0, 0, tiled=True)
    rows = rows.reshape(planes, nz // nl, 2, capacity, share).transpose(2, 1, 3, 0, 4)
    rows = rows.reshape(2 * nz // nl * capacity, planes * share)
    rows_peer = swap(rows, "c")

    same = yl == core
    rows_a, rows_b = jnp.where(same, rows, rows_peer), jnp.where(same, rows_peer, rows)
    basis_a = jnp.where(same, basis_half, basis_peer)
    basis_b = jnp.where(same, basis_peer, basis_half)
    part, act_sq = project(gathered, rows_a, rows_b, basis_a, basis_b, nl)
    act_sq = lax.all_gather(act_sq, "zl", axis=0, tiled=False)

    parts = lax.cond(
        lax.optimization_barrier(jnp.int32(1)) > 0,
        lambda x: lax.all_to_all(x, PLANE, 0, 0, tiled=True),
        lambda x: x,
        part.reshape(planes, nz * capacity // planes, -1),
    )
    grad_sq = jnp.square(jnp.sum(parts.astype(F32), axis=0)).astype(BF16)
    copies = jnp.broadcast_to(grad_sq[None], (planes,) + grad_sq.shape)
    grad_sq = lax.all_to_all(copies, PLANE, 0, 0, tiled=True).reshape(nz * capacity, -1)
    grad_sq_other = swap(grad_sq, "c")

    act_sq = act_sq.reshape(nl, 2, nz // nl * capacity, cols)

    def group(index):
        return lax.dynamic_index_in_dim(act_sq, index, 1, keepdims=False).reshape(nz * capacity, cols)

    act_first, act_second = group(core), group(1 - core)

    def outer(g, a):
        return lax.dot_general(g, a, (((0,), (0,)), ((), ())), preferred_element_type=F32)

    def block(lo, hi):
        own, other = grad_sq[:, lo:hi], grad_sq_other[:, lo:hi]
        return (outer(own, act_first) + outer(other, act_second)) / token_total

    keys = grad_sq.shape[1]
    got = swap(block(keys // 2, keys), "yl")
    kept = block(0, keys // 2)
    expert = lax.broadcasted_iota(jnp.int32, (2,) + kept.shape, 0)
    return jnp.where(expert == yl, kept[None], got[None])


def solution(mesh):
    dp, owner = mesh.devices.shape
    split = Mesh(
        mesh.devices.reshape(2, dp // 8, 4, 2, owner // 4, 2), ("yl", "zh", "zl", "yh", "x", "c")
    )
    rows, cols = ("yl", "zh", "zl"), ("yh", "x", "c")
    placed = (
        P(rows, None),
        P(None, rows, cols),
        P(None, cols, rows),
        P(None, rows, cols),
        P(rows, None),
    )
    return jax.shard_map(
        per_device, mesh=split, in_specs=placed, out_specs=P(None, rows, cols), check_vma=False
    )
```

```python
import jax
import jax.numpy as jnp
from jax import lax
from jax.experimental import pallas as pl
from jax.experimental.pallas import tpu as pltpu
from jax.sharding import Mesh, PartitionSpec as P

F32, BF16 = jnp.float32, jnp.bfloat16
PLANE = ("yh", "x")
VMEM_GRANT = 52


def pick_kernel(ids, grads, picked, chooser):
    experts, capacity, rows = chooser.shape
    first, second = ids[0:1, :], ids[1:2, :]
    source = lax.broadcasted_iota(jnp.int32, (rows, rows), 0)
    target = lax.broadcasted_iota(jnp.int32, (rows, rows), 1)
    before = (source <= target).astype(F32).astype(BF16)
    slot_order = lax.broadcasted_iota(jnp.int32, (capacity, rows), 0)
    for expert in range(experts):
        routed = jnp.logical_or(first == expert, second == expert)
        flags = jnp.broadcast_to(routed.astype(F32), (16, rows)).astype(BF16)
        slot_index = dot(flags, before)[0:1].astype(jnp.int32) - 1
        hit = jnp.logical_and(slot_order == slot_index, routed)
        chosen = hit.astype(F32).astype(BF16)
        chooser[expert] = chosen
        picked[expert] = dot(chosen, grads[expert]).astype(BF16)


def pick_grads(ids, grads, capacity):
    experts, rows, hidden = grads.shape
    return pl.pallas_call(
        pick_kernel,
        out_shape=[
            jax.ShapeDtypeStruct((experts, capacity, hidden), BF16),
            jax.ShapeDtypeStruct((experts, capacity, rows), BF16),
        ],
    )(ids.T, grads)


def swap(x, axis):
    return lax.ppermute(x, axis, [(0, 1), (1, 0)])


def dot(a, b):
    return jnp.dot(a, b, preferred_element_type=F32)


def project_kernel(got, rows, rows_peer, basis, basis_peer, part, act, total):
    step = pl.program_id(0)
    blocks, height, _ = got.shape
    cols = act.shape[1]
    deep, slots = height // 2, height // 4

    @pl.when(step == 0)
    def _():
        total[...] = jnp.zeros_like(total)

    grad = got[:, deep : deep + slots].reshape(blocks * slots, 2 * cols)
    grad_peer = got[:, deep + slots :].reshape(blocks * slots, 2 * cols)
    sums = dot(grad, basis[...]) + dot(grad_peer, basis_peer[...])
    sums = sums.astype(part.dtype).reshape((part.shape[1], part.shape[0]) + part.shape[2:])
    for group in range(part.shape[1]):
        part[:, group] = sums[group]
    own = got[:, :deep, :cols].reshape(blocks * deep, cols)
    other = got[:, :deep, cols:].reshape(blocks * deep, cols)
    total[...] += dot(rows[...], own) + dot(rows_peer[...], other)

    @pl.when(step == pl.num_programs(0) - 1)
    def _():
        rounded = total[...].astype(act.dtype).astype(F32)
        act[...] = (rounded * rounded).astype(act.dtype)


def project(got, rows, rows_peer, basis, basis_peer, blocks):
    nz, height, lanes = got.shape
    count, keys, cols = rows.shape[0], basis.shape[1], lanes // 2
    row_block = pl.BlockSpec((count, 2 * blocks * height // 2), lambda i: (0, i))
    whole = pl.BlockSpec(basis.shape, lambda i: (0, 0))
    made = nz * height // 4
    groups = 2
    step = groups * blocks
    return pl.pallas_call(
        project_kernel,
        grid=(nz // step,),
        in_specs=[
            pl.BlockSpec((step, height, lanes), lambda i: (i, 0, 0)),
            row_block,
            row_block,
            whole,
            whole,
        ],
        out_specs=[
            pl.BlockSpec((blocks, groups, height // 4, keys), lambda i: (0, i, 0, 0)),
            pl.BlockSpec((count, cols), lambda i: (0, 0)),
        ],
        out_shape=[
            jax.ShapeDtypeStruct((blocks, nz // blocks, height // 4, keys), BF16),
            jax.ShapeDtypeStruct((count, cols), BF16),
        ],
        scratch_shapes=[pltpu.VMEM((count, cols), F32)],
        compiler_params=pltpu.CompilerParams(vmem_limit_bytes=VMEM_GRANT * 1024 * 1024),
        cost_estimate=pl.CostEstimate(
            flops=4 * made * basis.shape[0] * keys + 4 * count * rows.shape[1] * cols,
            bytes_accessed=2 * (got.size + 2 * rows.size + 2 * basis.size + made * keys + count * cols),
            transcendentals=0,
        ),
    )(got, rows, rows_peer, basis, basis_peer)


def per_device(tokens, act_basis, grad_basis, grads, expert_ids):
    tok_rows, width = tokens.shape
    capacity = tok_rows // 2
    nl = lax.axis_size("zl")
    nz = lax.axis_size("zh") * nl
    token_total = tok_rows * lax.axis_size("yl") * nz
    planes = lax.axis_size("yh") * lax.axis_size("x")
    yl, core = lax.axis_index("yl"), lax.axis_index("c")
    cols = act_basis.shape[2]

    def mine(x):
        return lax.dynamic_index_in_dim(x, yl, 0, keepdims=False)

    def theirs(x):
        return lax.dynamic_index_in_dim(x, 1 - yl, 0, keepdims=False)

    act_other = swap(theirs(act_basis), "yl")
    picked_grad, choose = pick_grads(expert_ids, grads, capacity)
    straight = [(2 * y + c, 2 * c + y) for y in range(2) for c in range(2)]
    crossed = [(2 * y + c, 2 * (1 - c) + y) for y in range(2) for c in range(2)]
    grad_a = lax.ppermute(
        lax.dynamic_index_in_dim(picked_grad, core, 0, keepdims=False), ("yl", "c"), straight
    )
    grad_b = lax.ppermute(
        lax.dynamic_index_in_dim(picked_grad, 1 - core, 0, keepdims=False), ("yl", "c"), crossed
    )
    act_rows = jnp.concatenate([mine(act_basis), act_other], axis=1)
    payload = jnp.concatenate([act_rows, grad_a, grad_b], axis=0)
    gathered = lax.all_gather(payload, ("zh", "zl"), axis=0, tiled=False)

    plane = lax.axis_index("yh") * lax.axis_size("x") + lax.axis_index("x")
    share = width // (2 * planes)
    piece = lax.dynamic_slice_in_dim(tokens, core * (width // 2) + plane * share, share, 1)
    picked_act = jnp.stack([dot(choose[e], piece).astype(BF16) for e in range(2)])
    act_in, act_in_other = mine(picked_act), swap(theirs(picked_act), "yl")
    rows = jnp.concatenate(
        [jnp.where(yl == 0, act_in, act_in_other), jnp.where(yl == 0, act_in_other, act_in)], axis=0
    )
    rows = lax.all_gather(rows, "zh", axis=0, tiled=True)
    basis_half = jnp.concatenate([mine(grad_basis), swap(theirs(grad_basis), "yl")], axis=1)
    rows, basis_half = lax.optimization_barrier((rows, basis_half))
    basis_peer = swap(basis_half, "c")
    copies = jnp.broadcast_to(rows[None], (planes,) + rows.shape)
    rows = lax.all_to_all(copies, PLANE, 0, 0, tiled=True)
    rows = rows.reshape(planes, nz // nl, 2, capacity, share).transpose(2, 1, 3, 0, 4)
    rows = rows.reshape(2 * nz // nl * capacity, planes * share)
    rows_peer = swap(rows, "c")

    same = yl == core
    rows_a, rows_b = jnp.where(same, rows, rows_peer), jnp.where(same, rows_peer, rows)
    basis_a = jnp.where(same, basis_half, basis_peer)
    basis_b = jnp.where(same, basis_peer, basis_half)
    part, act_sq = project(gathered, rows_a, rows_b, basis_a, basis_b, nl)
    act_sq = lax.all_gather(act_sq, "zl", axis=0, tiled=False)

    parts = lax.cond(
        lax.optimization_barrier(jnp.int32(1)) > 0,
        lambda x: lax.all_to_all(x, PLANE, 0, 0, tiled=True),
        lambda x: x,
        part.reshape(planes, nz * capacity // planes, -1),
    )
    grad_sq = jnp.square(jnp.sum(parts.astype(F32), axis=0)).astype(BF16)
    copies = jnp.broadcast_to(grad_sq[None], (planes,) + grad_sq.shape)
    grad_sq = lax.all_to_all(copies, PLANE, 0, 0, tiled=True).reshape(nz * capacity, -1)
    grad_sq_other = swap(grad_sq, "c")

    act_sq = act_sq.reshape(nl, 2, nz // nl * capacity, cols)

    def group(index):
        return lax.dynamic_index_in_dim(act_sq, index, 1, keepdims=False).reshape(nz * capacity, cols)

    act_first, act_second = group(core), group(1 - core)

    def outer(g, a):
        return lax.dot_general(g, a, (((0,), (0,)), ((), ())), preferred_element_type=F32)

    def block(lo, hi):
        own, other = grad_sq[:, lo:hi], grad_sq_other[:, lo:hi]
        return (outer(own, act_first) + outer(other, act_second)) / token_total

    keys = grad_sq.shape[1]
    got = swap(block(keys // 2, keys), "yl")
    kept = block(0, keys // 2)
    expert = lax.broadcasted_iota(jnp.int32, (2,) + kept.shape, 0)
    return jnp.where(expert == yl, kept[None], got[None])


def solution(mesh):
    dp, owner = mesh.devices.shape
    split = Mesh(
        mesh.devices.reshape(2, dp // 8, 4, 2, owner // 4, 2), ("yl", "zh", "zl", "yh", "x", "c")
    )
    rows, cols = ("yl", "zh", "zl"), ("yh", "x", "c")
    placed = (
        P(rows, None),
        P(None, rows, cols),
        P(None, cols, rows),
        P(None, rows, cols),
        P(rows, None),
    )
    return jax.shard_map(
        per_device, mesh=split, in_specs=placed, out_specs=P(None, rows, cols), check_vma=False
    )
```

```python
import jax
import jax.numpy as jnp
from jax import lax
from jax.experimental import pallas as pl
from jax.experimental.pallas import tpu as pltpu
from jax.sharding import Mesh, PartitionSpec as P

F32, BF16 = jnp.float32, jnp.bfloat16
PLANE = ("yh", "x")
VMEM_GRANT = 52


def pick_kernel(ids, grads, picked, chooser):
    experts, capacity, rows = chooser.shape
    first, second = ids[0:1, :], ids[1:2, :]
    source = lax.broadcasted_iota(jnp.int32, (rows, rows), 0)
    target = lax.broadcasted_iota(jnp.int32, (rows, rows), 1)
    before = (source <= target).astype(F32).astype(BF16)
    slot_order = lax.broadcasted_iota(jnp.int32, (capacity, rows), 0)
    for expert in range(experts):
        routed = jnp.logical_or(first == expert, second == expert)
        flags = jnp.broadcast_to(routed.astype(F32), (16, rows)).astype(BF16)
        slot_index = dot(flags, before)[0:1].astype(jnp.int32) - 1
        hit = jnp.logical_and(slot_order == slot_index, routed)
        chosen = hit.astype(F32).astype(BF16)
        chooser[expert] = chosen
        picked[expert] = dot(chosen, grads[expert]).astype(BF16)


def pick_grads(ids, grads, capacity):
    experts, rows, hidden = grads.shape
    return pl.pallas_call(
        pick_kernel,
        out_shape=[
            jax.ShapeDtypeStruct((experts, capacity, hidden), BF16),
            jax.ShapeDtypeStruct((experts, capacity, rows), BF16),
        ],
    )(ids.T, grads)


def swap(x, axis):
    return lax.ppermute(x, axis, [(0, 1), (1, 0)])


def dot(a, b):
    return jnp.dot(a, b, preferred_element_type=F32)


def project_kernel(got, rows, rows_peer, basis, basis_peer, part, act, total):
    step = pl.program_id(0)
    blocks, height, _ = got.shape
    cols = act.shape[1]
    deep, slots = height // 2, height // 4

    @pl.when(step == 0)
    def _():
        total[...] = jnp.zeros_like(total)

    grad = got[:, deep : deep + slots].reshape(blocks * slots, 2 * cols)
    grad_peer = got[:, deep + slots :].reshape(blocks * slots, 2 * cols)
    sums = dot(grad, basis[...]) + dot(grad_peer, basis_peer[...])
    sums = sums.astype(part.dtype).reshape((part.shape[1], part.shape[0]) + part.shape[2:])
    for group in range(part.shape[1]):
        part[:, group] = sums[group]
    own = got[:, :deep, :cols].reshape(blocks * deep, cols)
    other = got[:, :deep, cols:].reshape(blocks * deep, cols)
    total[...] += dot(rows[...], own) + dot(rows_peer[...], other)

    @pl.when(step == pl.num_programs(0) - 1)
    def _():
        rounded = total[...].astype(act.dtype).astype(F32)
        act[...] = (rounded * rounded).astype(act.dtype)


def project(got, rows, rows_peer, basis, basis_peer, blocks):
    nz, height, lanes = got.shape
    count, keys, cols = rows.shape[0], basis.shape[1], lanes // 2
    row_block = pl.BlockSpec((count, 2 * blocks * height // 2), lambda i: (0, i))
    whole = pl.BlockSpec(basis.shape, lambda i: (0, 0))
    made = nz * height // 4
    groups = 2
    step = groups * blocks
    return pl.pallas_call(
        project_kernel,
        grid=(nz // step,),
        in_specs=[
            pl.BlockSpec((step, height, lanes), lambda i: (i, 0, 0)),
            row_block,
            row_block,
            whole,
            whole,
        ],
        out_specs=[
            pl.BlockSpec((blocks, groups, height // 4, keys), lambda i: (0, i, 0, 0)),
            pl.BlockSpec((count, cols), lambda i: (0, 0)),
        ],
        out_shape=[
            jax.ShapeDtypeStruct((blocks, nz // blocks, height // 4, keys), BF16),
            jax.ShapeDtypeStruct((count, cols), BF16),
        ],
        scratch_shapes=[pltpu.VMEM((count, cols), F32)],
        compiler_params=pltpu.CompilerParams(vmem_limit_bytes=VMEM_GRANT * 1024 * 1024),
        cost_estimate=pl.CostEstimate(
            flops=4 * made * basis.shape[0] * keys + 4 * count * rows.shape[1] * cols,
            bytes_accessed=2 * (got.size + 2 * rows.size + 2 * basis.size + made * keys + count * cols),
            transcendentals=0,
        ),
    )(got, rows, rows_peer, basis, basis_peer)


def per_device(tokens, act_basis, grad_basis, grads, expert_ids):
    tok_rows, width = tokens.shape
    capacity = tok_rows // 2
    nl = lax.axis_size("zl")
    nz = lax.axis_size("zh") * nl
    token_total = tok_rows * lax.axis_size("yl") * nz
    planes = lax.axis_size("yh") * lax.axis_size("x")
    yl, core = lax.axis_index("yl"), lax.axis_index("c")
    cols = act_basis.shape[2]

    def mine(x):
        return lax.dynamic_index_in_dim(x, yl, 0, keepdims=False)

    def theirs(x):
        return lax.dynamic_index_in_dim(x, 1 - yl, 0, keepdims=False)

    act_other = swap(theirs(act_basis), "yl")
    picked_grad, choose = pick_grads(expert_ids, grads, capacity)
    straight = [(2 * y + c, 2 * c + y) for y in range(2) for c in range(2)]
    crossed = [(2 * y + c, 2 * (1 - c) + y) for y in range(2) for c in range(2)]
    grad_a = lax.ppermute(
        lax.dynamic_index_in_dim(picked_grad, core, 0, keepdims=False), ("yl", "c"), straight
    )
    grad_b = lax.ppermute(
        lax.dynamic_index_in_dim(picked_grad, 1 - core, 0, keepdims=False), ("yl", "c"), crossed
    )
    act_rows = jnp.concatenate([mine(act_basis), act_other], axis=1)
    payload = jnp.concatenate([act_rows, grad_a, grad_b], axis=0)
    gathered = lax.all_gather(payload, ("zh", "zl"), axis=0, tiled=False)

    plane = lax.axis_index("yh") * lax.axis_size("x") + lax.axis_index("x")
    share = width // (2 * planes)
    piece = lax.dynamic_slice_in_dim(tokens, core * (width // 2) + plane * share, share, 1)
    picked_act = jnp.stack([dot(choose[e], piece).astype(BF16) for e in range(2)])
    act_in, act_in_other = mine(picked_act), swap(theirs(picked_act), "yl")
    rows = jnp.concatenate(
        [jnp.where(yl == 0, act_in, act_in_other), jnp.where(yl == 0, act_in_other, act_in)], axis=0
    )
    rows = lax.all_gather(rows, "zh", axis=0, tiled=True)
    basis_half = jnp.concatenate([mine(grad_basis), swap(theirs(grad_basis), "yl")], axis=1)
    rows, basis_half = lax.optimization_barrier((rows, basis_half))
    basis_peer = swap(basis_half, "c")
    copies = jnp.broadcast_to(rows[None], (planes,) + rows.shape)
    rows = lax.all_to_all(copies, PLANE, 0, 0, tiled=True)
    rows = rows.reshape(planes, nz // nl, 2, capacity, share).transpose(2, 1, 3, 0, 4)
    rows = rows.reshape(2 * nz // nl * capacity, planes * share)
    rows_peer = swap(rows, "c")

    same = yl == core
    rows_a, rows_b = jnp.where(same, rows, rows_peer), jnp.where(same, rows_peer, rows)
    basis_a = jnp.where(same, basis_half, basis_peer)
    basis_b = jnp.where(same, basis_peer, basis_half)
    part, act_sq = project(gathered, rows_a, rows_b, basis_a, basis_b, nl)
    act_sq = lax.all_gather(act_sq, "zl", axis=0, tiled=False)

    parts = lax.cond(
        lax.optimization_barrier(jnp.int32(1)) > 0,
        lambda x: lax.all_to_all(x, PLANE, 0, 0, tiled=True),
        lambda x: x,
        part.reshape(planes, nz * capacity // planes, -1),
    )
    grad_sq = jnp.square(jnp.sum(parts.astype(F32), axis=0)).astype(BF16)
    copies = jnp.broadcast_to(grad_sq[None], (planes,) + grad_sq.shape)
    grad_sq = lax.all_to_all(copies, PLANE, 0, 0, tiled=True).reshape(nz * capacity, -1)

    act_sq = act_sq.reshape(nl, 2, nz // nl * capacity, cols)

    def group(index):
        return lax.dynamic_index_in_dim(act_sq, index, 1, keepdims=False).reshape(nz * capacity, cols)

    act_first, act_second = group(core), group(1 - core)

    def outer(g, a):
        return lax.dot_general(g, a, (((0,), (0,)), ((), ())), preferred_element_type=F32)

    def block(lo, hi):
        own = grad_sq[:, lo:hi]
        other = swap(own, "c")
        return (outer(own, act_first) + outer(other, act_second)) / token_total

    keys = grad_sq.shape[1]
    got = swap(block(keys // 2, keys), "yl")
    kept = block(0, keys // 2)
    expert = lax.broadcasted_iota(jnp.int32, (2,) + kept.shape, 0)
    return jnp.where(expert == yl, kept[None], got[None])


def solution(mesh):
    dp, owner = mesh.devices.shape
    split = Mesh(
        mesh.devices.reshape(2, dp // 8, 4, 2, owner // 4, 2), ("yl", "zh", "zl", "yh", "x", "c")
    )
    rows, cols = ("yl", "zh", "zl"), ("yh", "x", "c")
    placed = (
        P(rows, None),
        P(None, rows, cols),
        P(None, cols, rows),
        P(None, rows, cols),
        P(rows, None),
    )
    return jax.shard_map(
        per_device, mesh=split, in_specs=placed, out_specs=P(None, rows, cols), check_vma=False
    )
```
